256 devices in a mesh: dp: 128 (over x, y, z), group: 2 (over core).
Axes of the slice: x: 4, y: 4, z: 8, core: 2. Of those that a mesh axis runs over, the one named last changes fastest.
Arguments:
- features: bfloat16 [32768, 32768], P(('dp', 'group')), may hold values from -6 to 6
- grad_slab: float32 [32768, 64], P('dp'), may hold values from -6 to 6
- damping: float32 [128], replicated, may hold values from 0.05 to 0.5
- owner_of: int32 [128], replicated, may hold values from 0 to 127, each once
Outputs:
- preconditioned: bfloat16 [32768, 64], replicated
The draws below stay inside these ranges and needn't reach their ends.
Inputs may be any that keep to these rules, and one draw needn't show every extreme that they name: `owner_of`: each dp index owns exactly one block.
All inputs are finite; a program needn't handle non-finite values. Where the reference program divides by a largest or mean magnitude, that divisor is 1e-20 or more.
Results may differ from the reference program's by a relative error of at most 0.0004.
Values may be sent and summed in bfloat16 or wider, within the bound.
A program may use at most 128 MiB of HBM per device.

```python
import math
import jax
import jax.numpy as jnp
from jax import lax

B = 256
COLS = 64
ITERS = 3
NBLK = 128
TOKENS = 32768


def block_levels(rng, extent, split, low, top_value):
    def one(dim, blocks):
        heights = jax.random.uniform(jax.random.fold_in(jax.random.fold_in(rng, 6), dim), (blocks,), jnp.float32, low / len(split), top_value / len(split))
        return jnp.repeat(jnp.exp(heights), extent[dim] // blocks).reshape((-1,) + (1,) * (len(extent) - dim - 1))

    loudness = one(*split[0])
    for cut in split[1:]:
        loudness = loudness * one(*cut)
    return loudness


def gaussian(own_key, shape, deviation, reach, split=(), kind=jnp.bfloat16):
    loudness = block_levels(own_key, shape, split, -0.22, 0.18) if split else 1.0
    values = jax.random.normal(own_key, shape, jnp.float32) * deviation * loudness
    return jnp.minimum(jnp.maximum(values, -reach), reach).astype(kind)


def setup_inputs(seed: int = 0) -> dict:
    key_of = jax.random.split(jax.random.key(seed), 5)
    features = gaussian(key_of[0], (TOKENS, NBLK * B), 1.0, 6.0, ((0, 256),))
    grad_slab = gaussian(key_of[1], (NBLK * B, COLS), 1.0, 6.0, ((0, 128),), jnp.float32)
    damping = jnp.clip(jnp.exp(jax.random.uniform(key_of[2], (NBLK,), jnp.float32, math.log(0.05), math.log(0.5))), 0.05, 0.5)
    owner_of = jax.random.permutation(key_of[3], NBLK).astype(jnp.int32)
    return {"features": features, "grad_slab": grad_slab, "damping": damping, "owner_of": owner_of}


def reference(features, grad_slab, damping, owner_of):
    nblk = damping.shape[0]
    eye = jnp.eye(B, dtype=jnp.float32)
    hi = lax.Precision.HIGHEST

    def one_block(index):
        cols = lax.dynamic_slice_in_dim(features, index * B, B, 1).astype(jnp.float32)
        cov = jnp.dot(cols.T, cols, precision=hi) / TOKENS
        mat = cov + damping[index] * eye
        alpha = 1.0 / jnp.max(jnp.sum(jnp.abs(mat), axis=1))
        inverse = alpha * eye
        for step in range(ITERS):
            inverse = 2.0 * inverse - jnp.dot(inverse, jnp.dot(mat, inverse, precision=hi), precision=hi)
        slab = lax.dynamic_slice_in_dim(grad_slab, owner_of[index].astype(jnp.int32) * B, B, 0)
        return jnp.dot(inverse, slab, precision=hi).astype(jnp.bfloat16)

    result = lax.map(one_block, jnp.arange(nblk, dtype=jnp.int32))
    return result.reshape(nblk * B, COLS)
```

```python
import jax
import jax.numpy as jnp
from jax import lax
from jax.experimental import pallas as pl
from jax.experimental.pallas import tpu as pltpu
from jax.sharding import PartitionSpec as P

B = 256
H = B // 2
COLS = 64
TOTAL = 32768
NX, NY, NZ = 4, 4, 8
NK = NZ // 2
OWNERS = NX * NY * NZ
ROWS = 128
HA = 64
HB = 72
F32 = jnp.float32
BF16 = jnp.bfloat16
MESH = pl.DeviceIdType.MESH


def order(i):
    return jnp.where(i == 0, 2, jnp.where(i == 3, 0, 2 * i - 1))


def dp_index(x, y, z):
    return (x * NY + y) * NZ + z


def reduce_kernel(
    slot_block, damping, features, slab_t, gathered,
    feat, xs, xr, pa, pb, tra, trb, pla, plb, sma, smb,
    l2sa, l2sb, l2ra, l2rb, l3s, l3r,
    feat_sem, ex_s, ex_r, l1_s, l1_r, l2_s, l2_r, l3_ss, l3_rs,
    ag1_s, ag1_r, ag2_s, ag3_s, ag_r, fw_s, fw_r,
):
    dp = lax.axis_index("dp")
    c = lax.axis_index("group")
    x = dp // (NY * NZ)
    y = (dp // NZ) % NY
    z = dp % NZ

    def load(b, carry):
        pltpu.make_async_copy(features.at[:, pl.ds(pl.multiple_of(b * B, B), B)], feat.at[b], feat_sem).start()
        return carry

    lax.fori_loop(0, OWNERS, load, 0)

    def at(xx, yy, zz, cc):
        return (dp_index(xx, yy, zz), cc)

    sibling = (dp, 1 - c)
    xnb = [at((x + d) % NX, y, z, c) for d in range(NX)]
    ynb = [at(x, (y + d) % NY, z, c) for d in range(NY)]
    znb = [at(x, y, (z + d) % NZ, c) for d in range(NZ)]

    barrier = pltpu.get_barrier_semaphore()
    peers = [sibling] + xnb[1:] + ynb[1:] + znb[1:]
    for peer in peers:
        pl.semaphore_signal(barrier, inc=1, device_id=peer, device_id_type=MESH)
    pl.semaphore_wait(barrier, len(peers))

    def remote(src, dst, s, r, dev):
        return pltpu.make_async_remote_copy(
            src_ref=src, dst_ref=dst, send_sem=s, recv_sem=r, device_id=dev, device_id_type=MESH
        )

    pltpu.make_async_copy(feat, feat, feat_sem).wait()

    def slot_of(dx, dy, k, cc):
        return dp_index((x + dx) % NX, (y + dy) % NY, 2 * k + cc)

    def block_of(dx, dy, k, cc):
        return feat[slot_block[slot_of(dx, dy, k, cc)]]

    def exchange(g, carry):
        dx, dy = order(g // 4), order(g % 4)
        for k in range(NK):
            xs[g, k] = block_of(dx, dy, k, 1 - c)
        remote(xs.at[g], xr.at[g], ex_s.at[g], ex_r.at[g], sibling).start()
        return carry

    lax.fori_loop(0, 16, exchange, 0)

    row = lax.broadcasted_iota(jnp.int32, (H, H), 0)
    col = lax.broadcasted_iota(jnp.int32, (H, H), 1)

    def level1(kind, axis, way, t):
        s, r = l1_s.at[kind, axis, way, t], l1_r.at[kind, axis, way, t]
        if axis == 0:
            src = {(0, 0): pa.at[2, t, 0], (0, 1): pa.at[2, t, 1], (1, 0): pa.at[1, t, 1], (1, 1): pa.at[3, t, 0],
                   (2, 0): pa.at[1, t, 0], (2, 1): pa.at[3, t, 1]}[kind, way]
            dst = (tra, pla, sma)[kind].at[way, t]
            dev = xnb[1 if way == 0 else 3]
        else:
            src = {(0, 0): pb.at[t, 2, 0], (0, 1): pb.at[t, 2, 1], (1, 0): pb.at[t, 1, 1], (1, 1): pb.at[t, 3, 0],
                   (2, 0): pb.at[t, 1, 0], (2, 1): pb.at[t, 3, 1]}[kind, way]
            dst = (trb, plb, smb)[kind].at[way, t]
            dev = ynb[1 if way == 0 else 3]
        return remote(src, dst, s, r, dev)

    def group(g, carry):
        dx, dy = order(g // 4), order(g % 4)
        remote(xs.at[g], xr.at[g], ex_s.at[g], ex_r.at[g], sibling).wait_recv()

        def slot(k, inner):
            own = block_of(dx, dy, k, c)
            f = jnp.concatenate([own, xr[g, k]], axis=0)
            t = lax.dot_general(f, f, (((0,), (0,)), ((), ())), preferred_element_type=F32)
            t00, t01, t11 = t[:H, :H], t[:H, H:], t[H:, H:]
            pa[dx, dy, 0, k] = t01[:HA]
            pa[dx, dy, 1, k] = t01[HA:]
            both = jnp.where(row < col, t00, t11)
            on = row == col
            d0 = jnp.sum(jnp.where(on, t00, 0.0), axis=0, keepdims=True)
            d1 = jnp.sum(jnp.where(on, t11, 0.0), axis=0, keepdims=True)
            pb[dx, dy, 0, k, :HA] = both[:HA]
            pb[dx, dy, 0, k, HA:] = jnp.broadcast_to(d0, (HB - HA, H))
            pb[dx, dy, 1, k, :HA] = both[HA:]
            pb[dx, dy, 1, k, HA:] = jnp.broadcast_to(d1, (HB - HA, H))
            return inner

        lax.fori_loop(0, NK, slot, 0)
        for axis, d, t in ((0, dx, dy), (1, dy, dx)):
            @pl.when(d == 2)
            def _():
                level1(0, axis, 0, t).start()
                level1(0, axis, 1, t).start()

            @pl.when(d == 1)
            def _():
                level1(1, axis, 0, t).start()

            @pl.when(d == 3)
            def _():
                level1(1, axis, 1, t).start()
        return carry

    lax.fori_loop(0, 16, group, 0)

    def pass_on(i, carry):
        t = order(i)
        for axis, p, tr in ((0, pa, tra), (1, pb, trb)):
            for way, d in ((0, 1), (1, 3)):
                level1(0, axis, way, t).wait_recv()
                ref = p.at[d, t, way] if axis == 0 else p.at[t, d, way]
                ref[...] = ref[...] + tr[way, t]
                level1(2, axis, way, t).start()
        return carry

    lax.fori_loop(0, 4, pass_on, 0)

    def level2(part, d):
        s, r = l2_s.at[part, d], l2_r.at[part, d]
        if part == 0:
            return remote(l2sa.at[d], l2ra.at[d], s, r, at(x, (y + d) % NY, z, c))
        return remote(l2sb.at[d], l2rb.at[d], s, r, at((x + d) % NX, y, z, c))

    def finish1(i, carry):
        t = order(i)
        for axis, p, plain, sums, out in ((0, pa, pla, sma, l2sa), (1, pb, plb, smb, l2sb)):
            for way in (0, 1):
                level1(1, axis, way, t).wait_recv()
                level1(2, axis, way, t).wait_recv()
            own = p.at[0, t] if axis == 0 else p.at[t, 0]
            out[t, 0] = own[0] + sums[0, t] + plain[1, t]
            out[t, 1] = own[1] + sums[1, t] + plain[0, t]

            @pl.when(t != 0)
            def _():
                level2(axis, t).start()
        return carry

    lax.fori_loop(0, 4, finish1, 0)

    for part, out, got, lo, size in ((0, l2sa, l2ra, 0, HA), (1, l2sb, l2rb, 2 * HA, HB)):
        for d in (1, 3, 2):
            level2(part, d).wait_recv()
        for h in (0, 1):
            l3s[:, lo + h * size : lo + (h + 1) * size] = out[0, h] + got[1, h] + got[2, h] + got[3, h]

    def level3(k):
        d = (2 * k + c - z + NZ) % NZ
        return remote(l3s.at[k], l3r.at[d], l3_ss.at[k], l3_rs.at[d], at(x, y, 2 * k + c, c))

    for k in range(NK):
        @pl.when(2 * k + c != z)
        def _():
            level3(k).start()

    owner = z % 2 == c
    xy = x * NY + y
    kz = z // 2

    def ag1(d):
        return remote(gathered.at[c, xy, kz], gathered.at[c, xy, kz], ag1_s.at[d], ag1_r.at[kz], znb[d])

    @pl.when(owner)
    def _():
        for d in range(1, NZ):
            pltpu.make_async_remote_copy(
                src_ref=l3r.at[d], dst_ref=l3r.at[d], send_sem=l3_ss.at[0], recv_sem=l3_rs.at[d],
                device_id=znb[d], device_id_type=MESH,
            ).wait_recv()
        total = l3s[kz]
        for d in range(1, NZ):
            total = total + l3r[d]
        scale = 1.0 / TOTAL
        t01 = total[: 2 * HA] * scale
        both = jnp.concatenate([total[2 * HA : 3 * HA], total[2 * HA + HB : 3 * HA + HB]], axis=0) * scale
        damp = damping[slot_block[dp]]
        d0 = total[3 * HA : 3 * HA + 1] * scale + damp
        d1 = total[3 * HA + HB : 3 * HA + HB + 1] * scale + damp
        flip = both.T
        t00 = jnp.where(row < col, both, jnp.where(row > col, flip, d0))
        t11 = jnp.where(row > col, both, jnp.where(row < col, flip, d1))
        mat = jnp.concatenate(
            [jnp.concatenate([t00, t01], axis=1), jnp.concatenate([t01.T, t11], axis=1)], axis=0
        )
        alpha = 1.0 / jnp.max(jnp.sum(jnp.abs(mat), axis=0, keepdims=True), axis=1, keepdims=True)

        def times(v):
            return jnp.dot(v, mat, precision=lax.Precision.HIGHEST, preferred_element_type=F32)

        def first(v):
            return 2.0 * alpha * v - alpha * alpha * times(v)

        def second(v):
            p = first(v)
            return 2.0 * p - first(times(p))

        v = second(slab_t[...])
        result = 2.0 * v - second(times(v))
        gathered[c, xy, kz] = result.astype(BF16)
        for d in range(1, NZ):
            ag1(d).start()

    for k in range(NK):
        @pl.when(2 * k + c != z)
        def _():
            pltpu.make_async_remote_copy(
                src_ref=gathered.at[c, xy, k], dst_ref=gathered.at[c, xy, k], send_sem=ag1_s.at[0], recv_sem=ag1_r.at[k],
                device_id=sibling, device_id_type=MESH,
            ).wait_recv()

    def bundle(cc, h, q):
        return gathered.at[cc, q, pl.ds(2 * h, 2)]

    def line(h, d):
        return x * NY + (y + d) % NY if h == 0 else ((x + d) % NX) * NY + y

    def ag2(h, d):
        dev = ynb[d] if h == 0 else xnb[d]
        return remote(bundle(c, h, xy), bundle(c, h, xy), ag2_s.at[h, d], ag_r.at[h, xy], dev)

    def ag3(h, e, d):
        q = line(h, e)
        dev = xnb[d] if h == 0 else ynb[d]
        return remote(bundle(c, h, q), bundle(c, h, q), ag3_s.at[h, e, d], ag_r.at[h, q], dev)

    def landed(h, q):
        remote(bundle(c, h, q), bundle(c, h, q), ag2_s.at[0, 0], ag_r.at[h, q], sibling).wait_recv()

    def forward(cc, h, q):
        return remote(bundle(cc, h, q), bundle(cc, h, q), fw_s.at[h, q], fw_r.at[h, q], sibling)

    for h in (0, 1):
        for d in (2, 1, 3):
            ag2(h, d).start()
    for h in (0, 1):
        for d in (2, 1, 3):
            ag3(h, 0, d).start()
        forward(c, h, xy).start()
    for e in (1, 3, 2):
        for h in (0, 1):
            landed(h, line(h, e))
            for d in (2, 1, 3):
                ag3(h, e, d).start()
            forward(c, h, line(h, e)).start()
    for e in (0, 1, 3, 2):
        for d in (1, 3, 2):
            for h in (0, 1):
                ex, ey = (d, e) if h == 0 else (e, d)
                q = ((x + ex) % NX) * NY + (y + ey) % NY
                landed(h, q)
                forward(c, h, q).start()

    def sent_exchange(g, carry):
        remote(xs.at[g], xr.at[g], ex_s.at[g], ex_r.at[g], sibling).wait_send()
        return carry

    lax.fori_loop(0, 16, sent_exchange, 0)

    def sent_level1(t, carry):
        for kind in range(3):
            for axis in (0, 1):
                for way in (0, 1):
                    level1(kind, axis, way, t).wait_send()
        return carry

    lax.fori_loop(0, 4, sent_level1, 0)
    for part in (0, 1):
        for d in (1, 2, 3):
            level2(part, d).wait_send()
    for k in range(NK):
        @pl.when(2 * k + c != z)
        def _():
            level3(k).wait_send()

    @pl.when(owner)
    def _():
        for d in range(1, NZ):
            ag1(d).wait_send()

    for h in (0, 1):
        for d in (1, 2, 3):
            ag2(h, d).wait_send()
            for e in range(4):
                ag3(h, e, d).wait_send()

    def sent_forward(q, carry):
        for h in (0, 1):
            forward(c, h, q).wait_send()
            forward(1 - c, h, q).wait_recv()
        return carry

    lax.fori_loop(0, 16, sent_forward, 0)


def permute_kernel(owner_of, gathered, out):
    def one(b, carry):
        o = owner_of[b]
        q, z = o // NZ, o % NZ
        out[:, pl.ds(pl.multiple_of(b * B, B), B)] = gathered[z % 2, q, z // 2]
        return carry

    lax.fori_loop(0, OWNERS, one, 0, unroll=4)


def shards(features, grad_slab, damping, owner_of):
    slots = jnp.arange(OWNERS, dtype=jnp.int32)
    slot_block = jnp.sum(jnp.where(owner_of[None, :] == slots[:, None], slots[None, :], 0), axis=1)
    vmem = pl.BlockSpec(memory_space=pltpu.VMEM)
    smem = pl.BlockSpec(memory_space=pltpu.SMEM)
    dma = pltpu.SemaphoreType.DMA
    gathered = pl.pallas_call(
        reduce_kernel,
        out_shape=jax.ShapeDtypeStruct((2, NX * NY, NK, COLS, B), BF16),
        in_specs=[smem, smem, pl.BlockSpec(memory_space=pl.ANY), vmem],
        out_specs=vmem,
        scratch_shapes=[
            pltpu.VMEM((OWNERS, ROWS, B), BF16),
            pltpu.VMEM((16, NK, ROWS, B), BF16),
            pltpu.VMEM((16, NK, ROWS, B), BF16),
            pltpu.VMEM((4, 4, 2, NK, HA, H), F32),
            pltpu.VMEM((4, 4, 2, NK, HB, H), F32),
            *[pltpu.VMEM((2, 4, NK, rows, H), F32) for _ in range(3) for rows in (HA, HB)],
            pltpu.VMEM((4, 2, NK, HA, H), F32),
            pltpu.VMEM((4, 2, NK, HB, H), F32),
            pltpu.VMEM((4, 2, NK, HA, H), F32),
            pltpu.VMEM((4, 2, NK, HB, H), F32),
            pltpu.VMEM((NK, 2 * (HA + HB), H), F32),
            pltpu.VMEM((NZ, 2 * (HA + HB), H), F32),
            dma,
            dma((16,)), dma((16,)),
            dma((3, 2, 2, 4)), dma((3, 2, 2, 4)),
            dma((2, 4)), dma((2, 4)),
            dma((NK,)), dma((NZ,)),
            dma((NZ,)), dma((NK,)),
            dma((2, 4)), dma((2, 4, 4)), dma((2, 16)),
            dma((2, 16)), dma((2, 16)),
        ],
        compiler_params=pltpu.CompilerParams(
            collective_id=0, has_side_effects=True, vmem_limit_bytes=58 * 1024 * 1024
        ),
    )(slot_block, damping, features, grad_slab.T)
    out = pl.pallas_call(
        permute_kernel,
        out_shape=jax.ShapeDtypeStruct((COLS, OWNERS * B), BF16),
        in_specs=[smem, vmem],
        out_specs=vmem,
        compiler_params=pltpu.CompilerParams(vmem_limit_bytes=32 * 1024 * 1024),
    )(owner_of, gathered)
    return out.T


def solution(mesh):
    return jax.shard_map(
        shards,
        mesh=mesh,
        in_specs=(P(("dp", "group"), None), P("dp", None), P(), P()),
        out_specs=P(),
        check_vma=False,
    )
```

```python
import jax
import jax.numpy as jnp
from jax import lax
from jax.experimental import pallas as pl
from jax.experimental.pallas import tpu as pltpu
from jax.sharding import PartitionSpec as P

B = 256
H = B // 2
COLS = 64
TOTAL = 32768
NX, NY, NZ = 4, 4, 8
NK = NZ // 2
OWNERS = NX * NY * NZ
ROWS = 128
HA = 64
HB = 72
CODED = 4 * HA + 16
F32 = jnp.float32
BF16 = jnp.bfloat16
MESH = pl.DeviceIdType.MESH


def order(i):
    return jnp.where(i == 0, 2, jnp.where(i == 3, 0, 2 * i - 1))


def dp_index(x, y, z):
    return (x * NY + y) * NZ + z


def encode(ref, parts, diagonals, tokens):
    unit = tokens // 512
    line = lax.broadcasted_iota(jnp.int32, (16, H), 0)
    extra = jnp.zeros((16, H), F32)
    for i, v in enumerate(parts):
        top = jnp.max(jnp.abs(v), axis=0, keepdims=True)
        units = jnp.maximum(jnp.ceil(top * (1.0 / unit)), 1.0)
        coded = jnp.round(v * ((32767.0 / unit) / units))
        ref[HA * i : HA * (i + 1)] = coded.astype(jnp.int32).astype(jnp.int16)
        extra = jnp.where(line == i, units, extra)
    for i, d in diagonals.items():
        scaled = d * (32767.0 / (36.0 * tokens))
        high = jnp.floor(scaled)
        low = jnp.round((scaled - high) * 32767.0)
        extra = jnp.where(line == 4 + i, high, jnp.where(line == 8 + i, low, extra))
    ref[4 * HA :] = extra.astype(jnp.int32).astype(jnp.int16)


def decode(ref, tokens):
    unit = tokens // 512
    extra = ref[4 * HA :].astype(jnp.int32).astype(F32)
    parts = []
    for i in range(4):
        v = ref[HA * i : HA * (i + 1)].astype(jnp.int32).astype(F32)
        parts.append(v * (extra[i : i + 1] * (unit / 32767.0)))
    rows = (extra[4:8] + extra[8:12] * (1.0 / 32767.0)) * (36.0 * tokens / 32767.0)
    return parts, [rows[i : i + 1] for i in range(4)]


def reduce_kernel(
    slot_block, damping, features, slab_t, gathered,
    feat, xs, xr, pa, pb, sent1, got1, sent2, got2, sent3, got3,
    feat_sem, ex_s, ex_r, l1_s, l1_r, l2_s, l2_r, l3_ss, l3_rs,
    ag1_s, ag1_r, ag2_s, ag3_s, ag_r, fw_s, fw_r,
):
    dp = lax.axis_index("dp")
    c = lax.axis_index("group")
    x = dp // (NY * NZ)
    y = (dp // NZ) % NY
    z = dp % NZ

    def load(b, carry):
        pltpu.make_async_copy(features.at[:, pl.ds(pl.multiple_of(b * B, B), B)], feat.at[b], feat_sem).start()
        return carry

    lax.fori_loop(0, OWNERS, load, 0)

    def at(xx, yy, zz, cc):
        return (dp_index(xx, yy, zz), cc)

    sibling = (dp, 1 - c)
    xnb = [at((x + d) % NX, y, z, c) for d in range(NX)]
    ynb = [at(x, (y + d) % NY, z, c) for d in range(NY)]
    znb = [at(x, y, (z + d) % NZ, c) for d in range(NZ)]

    barrier = pltpu.get_barrier_semaphore()
    peers = [sibling] + xnb[1:] + ynb[1:] + znb[1:]
    for peer in peers:
        pl.semaphore_signal(barrier, inc=1, device_id=peer, device_id_type=MESH)
    def remote(src, dst, s, r, dev):
        return pltpu.make_async_remote_copy(
            src_ref=src, dst_ref=dst, send_sem=s, recv_sem=r, device_id=dev, device_id_type=MESH
        )

    pltpu.make_async_copy(feat, feat, feat_sem).wait()

    def slot_of(dx, dy, k, cc):
        return dp_index((x + dx) % NX, (y + dy) % NY, 2 * k + cc)

    def block_of(dx, dy, k, cc):
        return feat[slot_block[slot_of(dx, dy, k, cc)]]

    def stage(g, carry):
        for k in range(NK):
            xs[g, k] = block_of(order(g // 4), order(g % 4), k, 1 - c)
        return carry

    lax.fori_loop(0, 16, stage, 0)
    pl.semaphore_wait(barrier, len(peers))

    def exchange(g, carry):
        remote(xs.at[g], xr.at[g], ex_s.at[g], ex_r.at[g], sibling).start()
        return carry

    lax.fori_loop(0, 16, exchange, 0)

    row = lax.broadcasted_iota(jnp.int32, (H, H), 0)
    col = lax.broadcasted_iota(jnp.int32, (H, H), 1)

    def level1(kind, axis, way, t):
        dev = (xnb, ynb)[axis][1 if way == 0 else 3]
        return remote(
            sent1.at[kind, axis, way, t], got1.at[kind, axis, way, t],
            l1_s.at[kind, axis, way, t], l1_r.at[kind, axis, way, t], dev,
        )

    def place(part, d, t):
        return pa.at[d, t] if part == 0 else pb.at[t, d]

    def pieces(ref, part, half):
        parts = [ref[half, k, :HA] for k in range(NK)]
        return parts, ({k: ref[half, k, HA : HA + 1] for k in range(NK)} if part == 1 else {})

    def send1(kind, part, d, half, way, t):
        parts, diagonals = pieces(place(part, d, t), part, half)
        encode(sent1.at[kind, part, way, t], parts, diagonals, 512)
        level1(kind, part, way, t).start()

    def group(g, carry):
        dx, dy = order(g // 4), order(g % 4)
        remote(xs.at[g], xr.at[g], ex_s.at[g], ex_r.at[g], sibling).wait_recv()

        for k in range(NK):
            own = block_of(dx, dy, k, c)
            f = jnp.concatenate([own, xr[g, k]], axis=0)
            t = lax.dot_general(f, f, (((0,), (0,)), ((), ())), preferred_element_type=F32)
            t00, t01, t11 = t[:H, :H], t[:H, H:], t[H:, H:]
            pa[dx, dy, 0, k] = t01[:HA]
            pa[dx, dy, 1, k] = t01[HA:]
            on = row == col
            both = jnp.where(row < col, t00, jnp.where(on, 0.0, t11))
            d0 = jnp.sum(jnp.where(on, t00, 0.0), axis=0, keepdims=True)
            d1 = jnp.sum(jnp.where(on, t11, 0.0), axis=0, keepdims=True)
            pb[dx, dy, 0, k, :HA] = both[:HA]
            pb[dx, dy, 0, k, HA:] = jnp.broadcast_to(d0, (HB - HA, H))
            pb[dx, dy, 1, k, :HA] = both[HA:]
            pb[dx, dy, 1, k, HA:] = jnp.broadcast_to(d1, (HB - HA, H))

        for part, d, t in ((0, dx, dy), (1, dy, dx)):
            @pl.when(d == 2)
            def _():
                send1(0, part, 2, 0, 0, t)
                send1(0, part, 2, 1, 1, t)

            @pl.when(d == 1)
            def _():
                send1(1, part, 1, 1, 0, t)

            @pl.when(d == 3)
            def _():
                send1(1, part, 3, 0, 1, t)
        return carry

    lax.fori_loop(0, 16, group, 0)

    def pass_on(i, carry):
        t = order(i)
        for part in (0, 1):
            for way, d in ((0, 1), (1, 3)):
                level1(0, part, way, t).wait_recv()
                parts, rows = decode(got1.at[0, part, way, t], 512)
                own, diagonals = pieces(place(part, d, t), part, way)
                parts = [a + b for a, b in zip(own, parts)]
                diagonals = {k: diagonals[k] + rows[k] for k in diagonals}
                encode(sent1.at[2, part, way, t], parts, diagonals, 512)
                level1(2, part, way, t).start()
        return carry

    lax.fori_loop(0, 4, pass_on, 0)

    def add_coded(ref, part, half, coded, tokens):
        for message in coded:
            parts, rows = decode(message, tokens)
            for k in range(NK):
                ref[half, k, :HA] = ref[half, k, :HA] + parts[k]
                if part == 1:
                    ref[half, k, HA:] = ref[half, k, HA:] + rows[k]

    def level2(part, d):
        dev = at(x, (y + d) % NY, z, c) if part == 0 else at((x + d) % NX, y, z, c)
        return remote(sent2.at[part, d], got2.at[part, d], l2_s.at[part, d], l2_r.at[part, d], dev)

    def finish1(i, carry):
        t = order(i)
        for part in (0, 1):
            for way in (0, 1):
                level1(1, part, way, t).wait_recv()
                level1(2, part, way, t).wait_recv()
            ref = place(part, 0, t)
            for half in (0, 1):
                add_coded(ref, part, half, (got1.at[2, part, half, t], got1.at[1, part, 1 - half, t]), 512)

            @pl.when(t != 0)
            def _():
                for half in (0, 1):
                    encode(sent2.at[part, t, half], *pieces(ref, part, half), 1024)
                level2(part, t).start()
        return carry

    lax.fori_loop(0, 4, finish1, 0)

    for part in (0, 1):
        for d in (1, 3, 2):
            level2(part, d).wait_recv()
            for half in (0, 1):
                add_coded(place(part, 0, 0), part, half, (got2.at[part, d, half],), 1024)

    def level3(k):
        d = (2 * k + c - z + NZ) % NZ
        return remote(sent3.at[k], got3.at[d], l3_ss.at[k], l3_rs.at[d], at(x, y, 2 * k + c, c))

    def send3(k, carry):
        @pl.when(2 * k + c != z)
        def _():
            parts = [pa[0, 0, 0, k], pa[0, 0, 1, k], pb[0, 0, 0, k, :HA], pb[0, 0, 1, k, :HA]]
            diagonals = {2: pb[0, 0, 0, k, HA : HA + 1], 3: pb[0, 0, 1, k, HA : HA + 1]}
            encode(sent3.at[k], parts, diagonals, 4096)
            level3(k).start()

        return carry

    lax.fori_loop(0, NK, send3, 0)

    owner = z % 2 == c
    xy = x * NY + y
    kz = z // 2

    def ag1(d):
        return remote(gathered.at[c, xy, kz], gathered.at[c, xy, kz], ag1_s.at[d], ag1_r.at[kz], znb[d])

    @pl.when(owner)
    def _():
        t01a, t01b = pa[0, 0, 0, kz], pa[0, 0, 1, kz]
        ba, bb = pb[0, 0, 0, kz, :HA], pb[0, 0, 1, kz, :HA]
        d0, d1 = pb[0, 0, 0, kz, HA : HA + 1], pb[0, 0, 1, kz, HA : HA + 1]
        for d in (1, 7, 2, 6, 3, 5, 4):
            remote(got3.at[d], got3.at[d], l3_ss.at[0], l3_rs.at[d], znb[d]).wait_recv()
            parts, rows = decode(got3.at[d], 4096)
            t01a, t01b, ba, bb = t01a + parts[0], t01b + parts[1], ba + parts[2], bb + parts[3]
            d0, d1 = d0 + rows[2], d1 + rows[3]
        scale = 1.0 / TOTAL
        t01 = jnp.concatenate([t01a, t01b], axis=0) * scale
        both = jnp.concatenate([ba, bb], axis=0) * scale
        damp = damping[slot_block[dp]]
        d0 = d0 * scale + damp
        d1 = d1 * scale + damp
        flip = both.T
        t00 = jnp.where(row < col, both, jnp.where(row > col, flip, d0))
        t11 = jnp.where(row > col, both, jnp.where(row < col, flip, d1))
        mat = jnp.concatenate(
            [jnp.concatenate([t00, t01], axis=1), jnp.concatenate([t01.T, t11], axis=1)], axis=0
        )
        alpha = 1.0 / jnp.max(jnp.sum(jnp.abs(mat), axis=0, keepdims=True), axis=1, keepdims=True)

        def times(v):
            return jnp.dot(v, mat, precision=lax.Precision.HIGHEST, preferred_element_type=F32)

        def first(v):
            return 2.0 * alpha * v - alpha * alpha * times(v)

        def second(v):
            p = first(v)
            return 2.0 * p - first(times(p))

        v = second(slab_t[...])
        result = 2.0 * v - second(times(v))
        gathered[c, xy, kz] = result.astype(BF16)
        for d in range(1, NZ):
            ag1(d).start()

    for k in range(NK):
        @pl.when(2 * k + c != z)
        def _():
            pltpu.make_async_remote_copy(
                src_ref=gathered.at[c, xy, k], dst_ref=gathered.at[c, xy, k], send_sem=ag1_s.at[0], recv_sem=ag1_r.at[k],
                device_id=sibling, device_id_type=MESH,
            ).wait_recv()

    def bundle(cc, h, q):
        return gathered.at[cc, q, pl.ds(2 * h, 2)]

    def line(h, d):
        return x * NY + (y + d) % NY if h == 0 else ((x + d) % NX) * NY + y

    def ag2(h, d):
        dev = ynb[d] if h == 0 else xnb[d]
        return remote(bundle(c, h, xy), bundle(c, h, xy), ag2_s.at[h, d], ag_r.at[h, xy], dev)

    def ag3(h, e, d):
        q = line(h, e)
        dev = xnb[d] if h == 0 else ynb[d]
        return remote(bundle(c, h, q), bundle(c, h, q), ag3_s.at[h, e, d], ag_r.at[h, q], dev)

    def landed(h, q):
        remote(bundle(c, h, q), bundle(c, h, q), ag2_s.at[0, 0], ag_r.at[h, q], sibling).wait_recv()

    def forward(cc, h, q):
        return remote(bundle(cc, h, q), bundle(cc, h, q), fw_s.at[h, q], fw_r.at[h, q], sibling)

    for h in (0, 1):
        for d in (2, 1, 3):
            ag2(h, d).start()
    for h in (0, 1):
        for d in (2, 1, 3):
            ag3(h, 0, d).start()
        forward(c, h, xy).start()
    for e in (1, 3, 2):
        for h in (0, 1):
            landed(h, line(h, e))
            for d in (2, 1, 3):
                ag3(h, e, d).start()
            forward(c, h, line(h, e)).start()
    for e in (0, 1, 3, 2):
        for d in (1, 3, 2):
            for h in (0, 1):
                ex, ey = (d, e) if h == 0 else (e, d)
                q = ((x + ex) % NX) * NY + (y + ey) % NY
                landed(h, q)
                forward(c, h, q).start()

    def sent_exchange(g, carry):
        remote(xs.at[g], xr.at[g], ex_s.at[g], ex_r.at[g], sibling).wait_send()
        return carry

    lax.fori_loop(0, 16, sent_exchange, 0)

    def sent_level1(t, carry):
        for kind in range(3):
            for axis in (0, 1):
                for way in (0, 1):
                    level1(kind, axis, way, t).wait_send()
        return carry

    lax.fori_loop(0, 4, sent_level1, 0)
    for part in (0, 1):
        for d in (1, 2, 3):
            level2(part, d).wait_send()
    for k in range(NK):
        @pl.when(2 * k + c != z)
        def _():
            level3(k).wait_send()

    @pl.when(owner)
    def _():
        for d in range(1, NZ):
            ag1(d).wait_send()

    for h in (0, 1):
        for d in (1, 2, 3):
            ag2(h, d).wait_send()
            for e in range(4):
                ag3(h, e, d).wait_send()

    def sent_forward(q, carry):
        for h in (0, 1):
            forward(c, h, q).wait_send()
            forward(1 - c, h, q).wait_recv()
        return carry

    lax.fori_loop(0, 16, sent_forward, 0)


def permute_kernel(owner_of, gathered, out, sem):
    def one(b, carry):
        o = owner_of[b]
        q, z = o // NZ, o % NZ
        pltpu.make_async_copy(
            gathered.at[z % 2, q, z // 2], out.at[:, pl.ds(pl.multiple_of(b * B, B), B)], sem
        ).start()
        return carry

    lax.fori_loop(0, OWNERS, one, 0, unroll=8)
    pltpu.make_async_copy(out, out, sem).wait()


def shards(features, grad_slab, damping, owner_of):
    slots = jnp.arange(OWNERS, dtype=jnp.int32)
    slot_block = jnp.sum(jnp.where(owner_of[None, :] == slots[:, None], slots[None, :], 0), axis=1)
    vmem = pl.BlockSpec(memory_space=pltpu.VMEM)
    smem = pl.BlockSpec(memory_space=pltpu.SMEM)
    dma = pltpu.SemaphoreType.DMA
    gathered = pl.pallas_call(
        reduce_kernel,
        out_shape=pltpu.VMEM((2, NX * NY, NK, COLS, B), BF16),
        in_specs=[smem, smem, pl.BlockSpec(memory_space=pl.ANY), vmem],
        out_specs=vmem,
        scratch_shapes=[
            pltpu.VMEM((OWNERS, ROWS, B), BF16),
            pltpu.VMEM((16, NK, ROWS, B), BF16),
            pltpu.VMEM((16, NK, ROWS, B), BF16),
            pltpu.VMEM((4, 4, 2, NK, HA, H), F32),
            pltpu.VMEM((4, 4, 2, NK, HB, H), F32),
            pltpu.VMEM((3, 2, 2, 4, CODED, H), jnp.int16),
            pltpu.VMEM((3, 2, 2, 4, CODED, H), jnp.int16),
            pltpu.VMEM((2, 4, 2, CODED, H), jnp.int16),
            pltpu.VMEM((2, 4, 2, CODED, H), jnp.int16),
            pltpu.VMEM((NK, CODED, H), jnp.int16),
            pltpu.VMEM((NZ, CODED, H), jnp.int16),
            dma,
            dma((16,)), dma((16,)),
            dma((3, 2, 2, 4)), dma((3, 2, 2, 4)),
            dma((2, 4)), dma((2, 4)),
            dma((NK,)), dma((NZ,)),
            dma((NZ,)), dma((NK,)),
            dma((2, 4)), dma((2, 4, 4)), dma((2, 16)),
            dma((2, 16)), dma((2, 16)),
        ],
        compiler_params=pltpu.CompilerParams(
            collective_id=0, has_side_effects=True, vmem_limit_bytes=58 * 1024 * 1024
        ),
    )(slot_block, damping, features, grad_slab.T)
    out = pl.pallas_call(
        permute_kernel,
        out_shape=jax.ShapeDtypeStruct((COLS, OWNERS * B), BF16),
        in_specs=[smem, vmem],
        out_specs=pl.BlockSpec(memory_space=pl.ANY),
        scratch_shapes=[dma],
        compiler_params=pltpu.CompilerParams(vmem_limit_bytes=32 * 1024 * 1024),
    )(owner_of, gathered)
    return out.T


def solution(mesh):
    return jax.shard_map(
        shards,
        mesh=mesh,
        in_specs=(P(("dp", "group"), None), P("dp", None), P(), P()),
        out_specs=P(),
        check_vma=False,
    )
```

```python
import jax
import jax.numpy as jnp
from jax import lax
from jax.experimental import pallas as pl
from jax.experimental.pallas import tpu as pltpu
from jax.sharding import PartitionSpec as P

B = 256
H = B // 2
COLS = 64
TOTAL = 32768
NX, NY, NZ = 4, 4, 8
NK = NZ // 2
OWNERS = NX * NY * NZ
ROWS = 128
AHEAD = 3
HA = 64
HB = 72
CODED = 4 * HA + 16
F32 = jnp.float32
BF16 = jnp.bfloat16
MESH = pl.DeviceIdType.MESH


def order(i):
    return jnp.where(i == 0, 2, jnp.where(i == 3, 0, 2 * i - 1))


def pick(g):
    r = jnp.maximum(g - 7, 0)
    even = g % 2 == 0
    dx = jnp.where(g < 7, jnp.where(even, 2, order((g + 1) // 2)), order(1 + r // 3))
    dy = jnp.where(g < 7, jnp.where(even, order(g // 2), 2), order(1 + r % 3))
    return dx, dy


def rank(z, c, k):
    away = (k - (z - c + NZ) // 2 % NK + NK) % NK
    return away + away // 2 - 2 * (away // 3)


def dp_index(x, y, z):
    return (x * NY + y) * NZ + z


def encode(ref, parts, diagonals, tokens):
    unit = tokens // 512
    line = lax.broadcasted_iota(jnp.int32, (16, H), 0)
    extra = jnp.zeros((16, H), F32)
    for i, v in enumerate(parts):
        top = jnp.max(jnp.abs(v), axis=0, keepdims=True)
        units = jnp.maximum(jnp.ceil(top * (1.0 / unit)), 1.0)
        coded = jnp.round(v * ((32767.0 / unit) / units))
        ref[HA * i : HA * (i + 1)] = coded.astype(jnp.int32).astype(jnp.int16)
        extra = jnp.where(line == i, units, extra)
    for i, d in diagonals.items():
        scaled = d * (32767.0 / (36.0 * tokens))
        high = jnp.floor(scaled)
        low = jnp.round((scaled - high) * 32767.0)
        extra = jnp.where(line == 4 + i, high, jnp.where(line == 8 + i, low, extra))
    ref[4 * HA :] = extra.astype(jnp.int32).astype(jnp.int16)


def decode(ref, tokens):
    unit = tokens // 512
    extra = ref[4 * HA :].astype(jnp.int32).astype(F32)
    parts = []
    for i in range(4):
        v = ref[HA * i : HA * (i + 1)].astype(jnp.int32).astype(F32)
        parts.append(v * (extra[i : i + 1] * (unit / 32767.0)))
    rows = (extra[4:8] + extra[8:12] * (1.0 / 32767.0)) * (36.0 * tokens / 32767.0)
    return parts, [rows[i : i + 1] for i in range(4)]


def reduce_kernel(
    owner_of, damping_in, features, slab_in, gathered,
    slot_block, damping, slab_t, table, feat, xs, xr, pa, pb, sent1, got1, sent2, got2, sent3, got3,
    small_sem, feat_sem, ex_s, ex_r, l1_s, l1_r, l2_s, l2_r, l3_ss, l3_rs,
    ag1_s, ag1_r, ag2_s, ag3_s, ag_r, fw_s, fw_r,
):
    dp = lax.axis_index("dp")
    c = lax.axis_index("group")
    x = dp // (NY * NZ)
    y = (dp // NZ) % NY
    z = dp % NZ

    def at(xx, yy, zz, cc):
        return (dp_index(xx, yy, zz), cc)

    sibling = (dp, 1 - c)
    xnb = [at((x + d) % NX, y, z, c) for d in range(NX)]
    ynb = [at(x, (y + d) % NY, z, c) for d in range(NY)]
    znb = [at(x, y, (z + d) % NZ, c) for d in range(NZ)]

    barrier = pltpu.get_barrier_semaphore()
    peers = [sibling] + xnb[1:] + ynb[1:] + znb[1:]
    for peer in peers:
        pl.semaphore_signal(barrier, inc=1, device_id=peer, device_id_type=MESH)
    small = [
        pltpu.make_async_copy(a, b, small_sem.at[i])
        for i, (a, b) in enumerate(((damping_in, damping), (slab_in, slab_t)))
    ]
    for copy in small:
        copy.start()

    def load(b, carry):
        pltpu.make_async_copy(features.at[:, pl.ds(pl.multiple_of(b * B, B), B)], feat.at[b], feat_sem).start()
        return carry

    lax.fori_loop(0, OWNERS, load, 0)

    def remote(src, dst, s, r, dev):
        return pltpu.make_async_remote_copy(
            src_ref=src, dst_ref=dst, send_sem=s, recv_sem=r, device_id=dev, device_id_type=MESH
        )

    row = lax.broadcasted_iota(jnp.int32, (H, H), 0)
    col = lax.broadcasted_iota(jnp.int32, (H, H), 1)
    owners = jnp.broadcast_to(owner_of[...].astype(F32), (OWNERS, OWNERS)).T
    held = jnp.where(owners == col.astype(F32), row, 0)
    table[...] = jnp.minimum(jnp.sum(held, axis=0, keepdims=True), OWNERS - 1)
    copy = pltpu.make_async_copy(table, slot_block, small_sem.at[2])
    copy.start()
    copy.wait()
    pltpu.make_async_copy(feat, feat, feat_sem).wait()
    for copy in small:
        copy.wait()

    def slot_of(dx, dy, k, cc):
        return dp_index((x + dx) % NX, (y + dy) % NY, 2 * k + cc)

    def block_of(dx, dy, k, cc):
        return feat[slot_block[0, slot_of(dx, dy, k, cc)]]

    def stage(g, carry):
        dx, dy = pick(g)
        for k in range(NK):
            xs[g, k] = block_of(dx, dy, k, 1 - c)
        return carry

    lax.fori_loop(0, 16, stage, 0)
    pl.semaphore_wait(barrier, len(peers))

    def exchange(g, carry):
        remote(xs.at[g], xr.at[g], ex_s.at[g], ex_r.at[g], sibling).start()
        return carry

    lax.fori_loop(0, AHEAD, exchange, 0)

    def level1(kind, axis, way, t):
        dev = (xnb, ynb)[axis][1 if way == 0 else 3]
        return remote(
            sent1.at[kind, axis, way, t], got1.at[kind, axis, way, t],
            l1_s.at[kind, axis, way, t], l1_r.at[kind, axis, way, t], dev,
        )

    def place(part, d, t):
        return pa.at[d, t] if part == 0 else pb.at[t, d]

    def pieces(ref, part, half):
        parts = [ref[half, k, :HA] for k in range(NK)]
        return parts, ({k: ref[half, k, HA : HA + 1] for k in range(NK)} if part == 1 else {})

    def send1(kind, part, d, half, way, t):
        parts, diagonals = pieces(place(part, d, t), part, half)
        encode(sent1.at[kind, part, way, t], parts, diagonals, 512)
        level1(kind, part, way, t).start()

    def group(g, carry):
        dx, dy = pick(g)

        @pl.when(g + AHEAD < 16)
        def _():
            exchange(g + AHEAD, 0)

        remote(xs.at[g], xr.at[g], ex_s.at[g], ex_r.at[g], sibling).wait_recv()

        for k in range(NK):
            own = block_of(dx, dy, k, c)
            f = jnp.concatenate([own, xr[g, k]], axis=0)
            t = lax.dot_general(f, f, (((0,), (0,)), ((), ())), preferred_element_type=F32)
            t00, t01, t11 = t[:H, :H], t[:H, H:], t[H:, H:]
            pa[dx, dy, 0, k] = t01[:HA]
            pa[dx, dy, 1, k] = t01[HA:]
            on = row == col
            both = jnp.where(row < col, t00, jnp.where(on, 0.0, t11))
            d0 = jnp.sum(jnp.where(on, t00, 0.0), axis=0, keepdims=True)
            d1 = jnp.sum(jnp.where(on, t11, 0.0), axis=0, keepdims=True)
            pb[dx, dy, 0, k, :HA] = both[:HA]
            pb[dx, dy, 0, k, HA:] = jnp.broadcast_to(d0, (HB - HA, H))
            pb[dx, dy, 1, k, :HA] = both[HA:]
            pb[dx, dy, 1, k, HA:] = jnp.broadcast_to(d1, (HB - HA, H))

        for part, d, t in ((0, dx, dy), (1, dy, dx)):
            @pl.when(d == 2)
            def _():
                send1(0, part, 2, 0, 0, t)
                send1(0, part, 2, 1, 1, t)

            @pl.when(d == 1)
            def _():
                send1(1, part, 1, 1, 0, t)

            @pl.when(d == 3)
            def _():
                send1(1, part, 3, 0, 1, t)
        return carry

    lax.fori_loop(0, 16, group, 0)

    def pass_on(i, carry):
        t = order(i)
        for part in (0, 1):
            for way, d in ((0, 1), (1, 3)):
                level1(0, part, way, t).wait_recv()
                parts, rows = decode(got1.at[0, part, way, t], 512)
                own, diagonals = pieces(place(part, d, t), part, way)
                parts = [a + b for a, b in zip(own, parts)]
                diagonals = {k: diagonals[k] + rows[k] for k in diagonals}
                encode(sent1.at[2, part, way, t], parts, diagonals, 512)
                level1(2, part, way, t).start()
        return carry

    lax.fori_loop(0, 4, pass_on, 0)

    def add_coded(ref, part, half, coded):
        for message in coded:
            parts, rows = decode(message, 512)
            for k in range(NK):
                ref[half, k, :HA] = ref[half, k, :HA] + parts[k]
                if part == 1:
                    ref[half, k, HA:] = ref[half, k, HA:] + rows[k]

    def level2(part, d, pair):
        dev = at(x, (y + d) % NY, z, c) if part == 0 else at((x + d) % NX, y, z, c)
        return remote(
            sent2.at[part, d, pair], got2.at[part, d, pair], l2_s.at[part, d, pair], l2_r.at[part, d, pair], dev
        )

    halves = [(half, n) for half in (0, 1) for n in (0, 1)]

    def far(pair, n):
        return ((z - c + NZ) // 2 + ((2, 3), (1, 0))[pair][n]) % NK

    def send2(part, t, pair):
        ref = place(part, 0, t)
        parts = [ref[half, far(pair, n), :HA] for half, n in halves]
        diagonals = {2 * half + n: ref[half, far(pair, n), HA : HA + 1] for half, n in halves} if part == 1 else {}
        encode(sent2.at[part, t, pair], parts, diagonals, 1024)
        level2(part, t, pair).start()

    def finish1(i, carry):
        t = order(i)
        for part in (0, 1):
            for way in (0, 1):
                level1(1, part, way, t).wait_recv()
                level1(2, part, way, t).wait_recv()
            ref = place(part, 0, t)
            for half in (0, 1):
                add_coded(ref, part, half, (got1.at[2, part, half, t], got1.at[1, part, 1 - half, t]))

            @pl.when(t != 0)
            def _():
                send2(part, t, 0)
        return carry

    lax.fori_loop(0, 4, finish1, 0)

    def second_pair(i, carry):
        for part in (0, 1):
            send2(part, order(i), 1)
        return carry

    lax.fori_loop(0, 3, second_pair, 0)

    def level3(k):
        d = (2 * k + c - z + NZ) % NZ
        return remote(sent3.at[k], got3.at[d], l3_ss.at[k], l3_rs.at[d], at(x, y, 2 * k + c, c))

    def send3(k):
        @pl.when(2 * k + c != z)
        def _():
            parts = [pa[0, 0, 0, k], pa[0, 0, 1, k], pb[0, 0, 0, k, :HA], pb[0, 0, 1, k, :HA]]
            diagonals = {2: pb[0, 0, 0, k, HA : HA + 1], 3: pb[0, 0, 1, k, HA : HA + 1]}
            encode(sent3.at[k], parts, diagonals, 4096)
            level3(k).start()

    for pair in (0, 1):
        for part in (0, 1):
            ref = place(part, 0, 0)
            for d in (1, 3, 2):
                level2(part, d, pair).wait_recv()
                parts, rows = decode(got2.at[part, d, pair], 1024)
                for half, n in halves:
                    k = far(pair, n)
                    ref[half, k, :HA] = ref[half, k, :HA] + parts[2 * half + n]
                    if part == 1:
                        ref[half, k, HA:] = ref[half, k, HA:] + rows[2 * half + n]
        for n in (0, 1):
            send3(far(pair, n))

    owner = z % 2 == c
    xy = x * NY + y
    kz = z // 2

    def ag1(d):
        j = rank((z + d) % NZ, c, kz)
        return remote(gathered.at[c, xy, 0], gathered.at[c, xy, j], ag1_s.at[d], ag1_r.at[j], znb[d])

    @pl.when(owner)
    def _():
        t01a, t01b = pa[0, 0, 0, kz], pa[0, 0, 1, kz]
        ba, bb = pb[0, 0, 0, kz, :HA], pb[0, 0, 1, kz, :HA]
        d0, d1 = pb[0, 0, 0, kz, HA : HA + 1], pb[0, 0, 1, kz, HA : HA + 1]
        for d in (1, 7, 2, 6, 3, 5, 4):
            remote(got3.at[d], got3.at[d], l3_ss.at[0], l3_rs.at[d], znb[d]).wait_recv()
            parts, rows = decode(got3.at[d], 4096)
            t01a, t01b, ba, bb = t01a + parts[0], t01b + parts[1], ba + parts[2], bb + parts[3]
            d0, d1 = d0 + rows[2], d1 + rows[3]
        scale = 1.0 / TOTAL
        t01 = jnp.concatenate([t01a, t01b], axis=0) * scale
        both = jnp.concatenate([ba, bb], axis=0) * scale
        damp = damping[slot_block[0, dp]]
        d0 = d0 * scale + damp
        d1 = d1 * scale + damp
        flip = both.T
        t00 = jnp.where(row < col, both, jnp.where(row > col, flip, d0))
        t11 = jnp.where(row > col, both, jnp.where(row < col, flip, d1))
        mat = jnp.concatenate(
            [jnp.concatenate([t00, t01], axis=1), jnp.concatenate([t01.T, t11], axis=1)], axis=0
        )
        alpha = 1.0 / jnp.max(jnp.sum(jnp.abs(mat), axis=0, keepdims=True), axis=1, keepdims=True)

        def times(v):
            return jnp.dot(v, mat, precision=lax.Precision.HIGHEST, preferred_element_type=F32)

        def first(v):
            return 2.0 * alpha * v - alpha * alpha * times(v)

        def second(v):
            p = first(v)
            return 2.0 * p - first(times(p))

        v = second(slab_t[...])
        result = 2.0 * v - second(times(v))
        gathered[c, xy, 0] = result.astype(BF16)
        for d in (1, 7, 4, 3, 5, 2, 6):
            ag1(d).start()

    def along(j, e, d):
        ex, ey = (d, e) if j % 2 == 0 else (e, d)
        return ((x + ex) % NX) * NY + (y + ey) % NY

    def first_line(j):
        return ynb if j % 2 == 0 else xnb

    def last_line(j):
        return xnb if j % 2 == 0 else ynb

    def whole(j, q, s, r, dev):
        return remote(gathered.at[c, q, j], gathered.at[c, q, j], s, r, dev)

    def ag2(j, d):
        return whole(j, xy, ag2_s.at[j, d], ag_r.at[j, xy], first_line(j)[d])

    def ag3(j, e, d):
        q = along(j, e, 0)
        return whole(j, q, ag3_s.at[j, e, d], ag_r.at[j, q], last_line(j)[d])

    def landed(j, q):
        whole(j, q, ag2_s.at[0, 0], ag_r.at[j, q], sibling).wait_recv()

    def forward(cc, j, q):
        return remote(gathered.at[cc, q, j], gathered.at[cc, q, j], fw_s.at[j, q], fw_r.at[j, q], sibling)

    def pass1(j):
        def arrive():
            whole(j, xy, ag1_s.at[0], ag1_r.at[j], sibling).wait_recv()

        if j == 0:
            pl.when(jnp.logical_not(owner))(arrive)
        else:
            arrive()
        for d in (2, 1, 3):
            ag2(j, d).start()
        for d in (2, 1, 3):
            ag3(j, 0, d).start()
        forward(c, j, xy).start()

    def pass2(j):
        for e in (1, 3, 2):
            q = along(j, e, 0)
            landed(j, q)
            for d in (2, 1, 3):
                ag3(j, e, d).start()
            forward(c, j, q).start()

    def pass3(j):
        for e in (0, 1, 3, 2):
            for d in (1, 3, 2):
                q = along(j, e, d)
                landed(j, q)
                forward(c, j, q).start()

    for j in range(NK):
        pass1(j)
    for j in range(NK):
        pass2(j)
    for j in range(NK):
        pass3(j)

    def sent_exchange(g, carry):
        remote(xs.at[g], xr.at[g], ex_s.at[g], ex_r.at[g], sibling).wait_send()
        return carry

    lax.fori_loop(0, 16, sent_exchange, 0)

    def sent_level1(t, carry):
        for kind in range(3):
            for axis in (0, 1):
                for way in (0, 1):
                    level1(kind, axis, way, t).wait_send()
        return carry

    lax.fori_loop(0, 4, sent_level1, 0)
    for part in (0, 1):
        for d in (1, 2, 3):
            for pair in (0, 1):
                level2(part, d, pair).wait_send()
    for k in range(NK):
        @pl.when(2 * k + c != z)
        def _():
            level3(k).wait_send()

    @pl.when(owner)
    def _():
        for d in range(1, NZ):
            ag1(d).wait_send()

    for j in range(NK):
        for d in (1, 2, 3):
            ag2(j, d).wait_send()
            for e in range(4):
                ag3(j, e, d).wait_send()

    def sent_forward(q, carry):
        for j in range(NK):
            forward(c, j, q).wait_send()
            forward(1 - c, j, q).wait_recv()
        return carry

    lax.fori_loop(0, 16, sent_forward, 0)


def permute_kernel(owner_of, gathered, out, sem):
    here = lax.axis_index("dp") % NZ
    nearest = [lax.shift_right_logical(here - plane + NZ, 1) & (NK - 1) for plane in (0, 1)]

    def one(b, carry):
        o = owner_of[b]
        q, plane = lax.shift_right_logical(o, 3), o & 1
        away = (lax.shift_right_logical(o, 1) - jnp.where(plane == 0, *nearest)) & (NK - 1)
        j = away ^ lax.shift_right_logical(away, 1)
        pltpu.make_async_copy(
            gathered.at[plane, q, j], out.at[:, pl.ds(pl.multiple_of(b * B, B), B)], sem
        ).start()
        return carry

    lax.fori_loop(0, OWNERS, one, 0, unroll=8)
    pltpu.make_async_copy(out, out, sem).wait()


def shards(features, grad_slab, damping, owner_of):
    vmem = pl.BlockSpec(memory_space=pltpu.VMEM)
    smem = pl.BlockSpec(memory_space=pltpu.SMEM)
    dma = pltpu.SemaphoreType.DMA
    gathered = pl.pallas_call(
        reduce_kernel,
        out_shape=pltpu.VMEM((2, NX * NY, NK, COLS, B), BF16),
        in_specs=[vmem] + [pl.BlockSpec(memory_space=pl.ANY)] * 3,
        out_specs=vmem,
        scratch_shapes=[
            pltpu.SMEM((1, OWNERS), jnp.int32),
            pltpu.SMEM((OWNERS,), F32),
            pltpu.VMEM((COLS, B), F32),
            pltpu.VMEM((1, OWNERS), jnp.int32),
            pltpu.VMEM((OWNERS, ROWS, B), BF16),
            pltpu.VMEM((16, NK, ROWS, B), BF16),
            pltpu.VMEM((16, NK, ROWS, B), BF16),
            pltpu.VMEM((4, 4, 2, NK, HA, H), F32),
            pltpu.VMEM((4, 4, 2, NK, HB, H), F32),
            pltpu.VMEM((3, 2, 2, 4, CODED, H), jnp.int16),
            pltpu.VMEM((3, 2, 2, 4, CODED, H), jnp.int16),
            pltpu.VMEM((2, 4, 2, CODED, H), jnp.int16),
            pltpu.VMEM((2, 4, 2, CODED, H), jnp.int16),
            pltpu.VMEM((NK, CODED, H), jnp.int16),
            pltpu.VMEM((NZ, CODED, H), jnp.int16),
            dma((3,)), dma,
            dma((16,)), dma((16,)),
            dma((3, 2, 2, 4)), dma((3, 2, 2, 4)),
            dma((2, 4, 2)), dma((2, 4, 2)),
            dma((NK,)), dma((NZ,)),
            dma((NZ,)), dma((NK,)),
            dma((NK, 4)), dma((NK, 4, 4)), dma((NK, 16)),
            dma((NK, 16)), dma((NK, 16)),
        ],
        compiler_params=pltpu.CompilerParams(
            collective_id=0, has_side_effects=True, vmem_limit_bytes=58 * 1024 * 1024
        ),
    )(owner_of.reshape(1, OWNERS), damping, features, grad_slab.T)
    out = pl.pallas_call(
        permute_kernel,
        out_shape=jax.ShapeDtypeStruct((COLS, OWNERS * B), BF16),
        in_specs=[smem, vmem],
        out_specs=pl.BlockSpec(memory_space=pl.ANY),
        scratch_shapes=[dma],
        compiler_params=pltpu.CompilerParams(vmem_limit_bytes=32 * 1024 * 1024),
    )(owner_of, gathered)
    return out.T


def solution(mesh):
    return jax.shard_map(
        shards,
        mesh=mesh,
        in_specs=(P(("dp", "group"), None), P("dp", None), P(), P()),
        out_specs=P(),
        check_vma=False,
    )
```

```python
import jax
import jax.numpy as jnp
from jax import lax
from jax.experimental import pallas as pl
from jax.experimental.pallas import tpu as pltpu
from jax.sharding import PartitionSpec as P

B = 256
H = B // 2
COLS = 64
TOTAL = 32768
NX, NY, NZ = 4, 4, 8
NK = NZ // 2
OWNERS = NX * NY * NZ
ROWS = 128
AHEAD = 5
HA = 64
HB = 72
CODED = 4 * HA + 16
F32 = jnp.float32
BF16 = jnp.bfloat16
MESH = pl.DeviceIdType.MESH


def order(i):
    return jnp.where(i == 0, 2, jnp.where(i == 3, 0, 2 * i - 1))


def pick(g):
    r = jnp.maximum(g - 7, 0)
    even = g % 2 == 0
    dx = jnp.where(g < 7, jnp.where(even, 2, order((g + 1) // 2)), order(1 + r // 3))
    dy = jnp.where(g < 7, jnp.where(even, order(g // 2), 2), order(1 + r % 3))
    return dx, dy


def rank(z, c, k):
    away = (k - (z - c + NZ) // 2 % NK + NK) % NK
    return away + away // 2 - 2 * (away // 3)


def dp_index(x, y, z):
    return (x * NY + y) * NZ + z


def encode(ref, parts, diagonals, tokens):
    unit = tokens // 512
    line = lax.broadcasted_iota(jnp.int32, (16, H), 0)
    extra = jnp.zeros((16, H), F32)
    for i, v in enumerate(parts):
        top = jnp.max(jnp.abs(v), axis=0, keepdims=True)
        units = jnp.maximum(jnp.ceil(top * (1.0 / unit)), 1.0)
        coded = jnp.round(v * ((32767.0 / unit) / units))
        ref[HA * i : HA * (i + 1)] = coded.astype(jnp.int32).astype(jnp.int16)
        extra = jnp.where(line == i, units, extra)
    for i, d in diagonals.items():
        scaled = d * (32767.0 / (36.0 * tokens))
        high = jnp.floor(scaled)
        low = jnp.round((scaled - high) * 32767.0)
        extra = jnp.where(line == 4 + i, high, jnp.where(line == 8 + i, low, extra))
    ref[4 * HA :] = extra.astype(jnp.int32).astype(jnp.int16)


def decode(ref, tokens):
    unit = tokens // 512
    extra = ref[4 * HA :].astype(jnp.int32).astype(F32)
    parts = []
    for i in range(4):
        v = ref[HA * i : HA * (i + 1)].astype(jnp.int32).astype(F32)
        parts.append(v * (extra[i : i + 1] * (unit / 32767.0)))
    rows = (extra[4:8] + extra[8:12] * (1.0 / 32767.0)) * (36.0 * tokens / 32767.0)
    return parts, [rows[i : i + 1] for i in range(4)]


def reduce_kernel(
    owner_of, damping_in, features, slab_in, gathered,
    slot_block, damping, slab_t, table, feat, xs, xr, pa, pb, sent1, got1, sent2, got2, sent3, got3,
    turn, small_sem, feat_sem, ex_s, ex_r, l1_s, l1_r, l2_s, l2_r, l3_ss, l3_rs,
    ag1_s, ag1_r, ag2_s, ag3_s, ag_r, fw_s, fw_r,
):
    dp = lax.axis_index("dp")
    c = lax.axis_index("group")
    x = dp // (NY * NZ)
    y = (dp // NZ) % NY
    z = dp % NZ

    def at(xx, yy, zz, cc):
        return (dp_index(xx, yy, zz), cc)

    sibling = (dp, 1 - c)
    xnb = [at((x + d) % NX, y, z, c) for d in range(NX)]
    ynb = [at(x, (y + d) % NY, z, c) for d in range(NY)]
    znb = [at(x, y, (z + d) % NZ, c) for d in range(NZ)]

    barrier = pltpu.get_barrier_semaphore()
    peers = [sibling] + xnb[1:] + ynb[1:] + znb[1:]
    for peer in peers:
        pl.semaphore_signal(barrier, inc=1, device_id=peer, device_id_type=MESH)
    small = [
        pltpu.make_async_copy(a, b, small_sem.at[i])
        for i, (a, b) in enumerate(((damping_in, damping), (slab_in, slab_t)))
    ]
    for copy in small:
        copy.start()

    def load(b, carry):
        pltpu.make_async_copy(features.at[:, pl.ds(pl.multiple_of(b * B, B), B)], feat.at[b], feat_sem).start()
        return carry

    lax.fori_loop(0, OWNERS, load, 0)

    def remote(src, dst, s, r, dev):
        return pltpu.make_async_remote_copy(
            src_ref=src, dst_ref=dst, send_sem=s, recv_sem=r, device_id=dev, device_id_type=MESH
        )

    row = lax.broadcasted_iota(jnp.int32, (H, H), 0)
    col = lax.broadcasted_iota(jnp.int32, (H, H), 1)
    owners = jnp.broadcast_to(owner_of[...].astype(F32), (OWNERS, OWNERS)).T
    held = jnp.where(owners == col.astype(F32), row, 0)
    table[...] = jnp.minimum(jnp.sum(held, axis=0, keepdims=True), OWNERS - 1)
    copy = pltpu.make_async_copy(table, slot_block, small_sem.at[2])
    copy.start()
    copy.wait()
    pltpu.make_async_copy(feat, feat, feat_sem).wait()
    for copy in small:
        copy.wait()

    def slot_of(dx, dy, k, cc):
        return dp_index((x + dx) % NX, (y + dy) % NY, 2 * k + cc)

    def block_of(dx, dy, k, cc):
        return feat[slot_block[0, slot_of(dx, dy, k, cc)]]

    def stage(g, carry):
        dx, dy = pick(g)
        for k in range(NK):
            xs[g, k] = block_of(dx, dy, k, 1 - c)
        return carry

    lax.fori_loop(0, AHEAD, stage, 0)
    pl.semaphore_wait(barrier, len(peers))

    def exchange(g, carry):
        remote(xs.at[g], xr.at[g], ex_s.at[g], ex_r.at[g], sibling).start()
        return carry

    lax.fori_loop(0, AHEAD, exchange, 0)

    def level1(kind, axis, way, t):
        dev = (xnb, ynb)[axis][1 if way == 0 else 3]
        return remote(
            sent1.at[kind, axis, way, t], got1.at[kind, axis, way, t],
            l1_s.at[kind, axis, way, t], l1_r.at[kind, axis, way, t], dev,
        )

    def place(part, d, t):
        return pa.at[d, t] if part == 0 else pb.at[t, d]

    def pieces(ref, part, half):
        parts = [ref[half, k, :HA] for k in range(NK)]
        return parts, ({k: ref[half, k, HA : HA + 1] for k in range(NK)} if part == 1 else {})

    def send1(kind, part, d, half, way, t):
        parts, diagonals = pieces(place(part, d, t), part, half)
        encode(sent1.at[kind, part, way, t], parts, diagonals, 512)

        @pl.when(c == 0)
        def _():
            level1(kind, part, way, t).start()

    def group(g, carry):
        dx, dy = pick(g)

        @pl.when(g + AHEAD < 16)
        def _():
            stage(g + AHEAD, 0)
            exchange(g + AHEAD, 0)

        remote(xs.at[g], xr.at[g], ex_s.at[g], ex_r.at[g], sibling).wait_recv()

        for k in range(NK):
            own = block_of(dx, dy, k, c)
            f = jnp.concatenate([own, xr[g, k]], axis=0)
            t = lax.dot_general(f, f, (((0,), (0,)), ((), ())), preferred_element_type=F32)
            t00, t01, t11 = t[:H, :H], t[:H, H:], t[H:, H:]
            pa[dx, dy, 0, k] = t01[:HA]
            pa[dx, dy, 1, k] = t01[HA:]
            on = row == col
            both = jnp.where(row < col, t00, jnp.where(on, 0.0, t11))
            d0 = jnp.sum(jnp.where(on, t00, 0.0), axis=0, keepdims=True)
            d1 = jnp.sum(jnp.where(on, t11, 0.0), axis=0, keepdims=True)
            pb[dx, dy, 0, k, :HA] = both[:HA]
            pb[dx, dy, 0, k, HA:] = jnp.broadcast_to(d0, (HB - HA, H))
            pb[dx, dy, 1, k, :HA] = both[HA:]
            pb[dx, dy, 1, k, HA:] = jnp.broadcast_to(d1, (HB - HA, H))

        for part, d, t in ((0, dx, dy), (1, dy, dx)):
            @pl.when(d == 2)
            def _():
                send1(0, part, 2, 0, 0, t)
                send1(0, part, 2, 1, 1, t)

            @pl.when(d == 1)
            def _():
                send1(1, part, 1, 1, 0, t)

            @pl.when(d == 3)
            def _():
                send1(1, part, 3, 0, 1, t)
        return carry

    lax.fori_loop(0, 16, group, 0)

    def each1(kinds, action):
        def step(i, carry):
            for kind in kinds:
                for part in (0, 1):
                    for way in (0, 1):
                        action(level1(kind, part, way, order(i)))
            return carry

        lax.fori_loop(0, 4, step, 0)

    @pl.when(c == 1)
    def _():
        pl.semaphore_wait(turn, 1)
        each1((0,), lambda copy: copy.start())
        each1((1,), lambda copy: copy.start())

    def pass_on(i, carry):
        t = order(i)
        for part in (0, 1):
            for way, d in ((0, 1), (1, 3)):
                level1(0, part, way, t).wait_recv()
                parts, rows = decode(got1.at[0, part, way, t], 512)
                own, diagonals = pieces(place(part, d, t), part, way)
                parts = [a + b for a, b in zip(own, parts)]
                diagonals = {k: diagonals[k] + rows[k] for k in diagonals}
                encode(sent1.at[2, part, way, t], parts, diagonals, 512)
                level1(2, part, way, t).start()
        return carry

    lax.fori_loop(0, 4, pass_on, 0)

    def add_coded(ref, part, half, coded):
        for message in coded:
            parts, rows = decode(message, 512)
            for k in range(NK):
                ref[half, k, :HA] = ref[half, k, :HA] + parts[k]
                if part == 1:
                    ref[half, k, HA:] = ref[half, k, HA:] + rows[k]

    def level2(part, d, pair):
        dev = at(x, (y + d) % NY, z, c) if part == 0 else at((x + d) % NX, y, z, c)
        return remote(
            sent2.at[part, d, pair], got2.at[part, d, pair], l2_s.at[part, d, pair], l2_r.at[part, d, pair], dev
        )

    halves = [(half, n) for half in (0, 1) for n in (0, 1)]

    def far(pair, n):
        return ((z - c + NZ) // 2 + ((2, 3), (1, 0))[pair][n]) % NK

    def send2(part, t, pair):
        ref = place(part, 0, t)
        parts = [ref[half, far(pair, n), :HA] for half, n in halves]
        diagonals = {2 * half + n: ref[half, far(pair, n), HA : HA + 1] for half, n in halves} if part == 1 else {}
        encode(sent2.at[part, t, pair], parts, diagonals, 1024)
        level2(part, t, pair).start()

    def finish1(i, carry):
        t = order(i)
        for part in (0, 1):
            for way in (0, 1):
                level1(1, part, way, t).wait_recv()
                level1(2, part, way, t).wait_recv()
            ref = place(part, 0, t)
            for half in (0, 1):
                add_coded(ref, part, half, (got1.at[2, part, half, t], got1.at[1, part, 1 - half, t]))

            @pl.when(t != 0)
            def _():
                send2(part, t, 0)
        return carry

    lax.fori_loop(0, 4, finish1, 0)

    @pl.when(c == 0)
    def _():
        each1((0, 1), lambda copy: copy.wait_send())
        pl.semaphore_signal(turn, inc=1, device_id=sibling, device_id_type=MESH)

    def second_pair(i, carry):
        for part in (0, 1):
            send2(part, order(i), 1)
        return carry

    lax.fori_loop(0, 3, second_pair, 0)

    def level3(k):
        d = (2 * k + c - z + NZ) % NZ
        return remote(sent3.at[k], got3.at[d], l3_ss.at[k], l3_rs.at[d], at(x, y, 2 * k + c, c))

    def send3(k):
        @pl.when(2 * k + c != z)
        def _():
            parts = [pa[0, 0, 0, k], pa[0, 0, 1, k], pb[0, 0, 0, k, :HA], pb[0, 0, 1, k, :HA]]
            diagonals = {2: pb[0, 0, 0, k, HA : HA + 1], 3: pb[0, 0, 1, k, HA : HA + 1]}
            encode(sent3.at[k], parts, diagonals, 4096)
            level3(k).start()

    for pair in (0, 1):
        for part in (0, 1):
            ref = place(part, 0, 0)
            for d in (1, 3, 2):
                level2(part, d, pair).wait_recv()
                parts, rows = decode(got2.at[part, d, pair], 1024)
                for half, n in halves:
                    k = far(pair, n)
                    ref[half, k, :HA] = ref[half, k, :HA] + parts[2 * half + n]
                    if part == 1:
                        ref[half, k, HA:] = ref[half, k, HA:] + rows[2 * half + n]
        for n in (0, 1):
            send3(far(pair, n))

    owner = z % 2 == c
    xy = x * NY + y
    kz = z // 2

    def ag1(d):
        j = rank((z + d) % NZ, c, kz)
        return remote(gathered.at[c, xy, 0], gathered.at[c, xy, j], ag1_s.at[d], ag1_r.at[j], znb[d])

    @pl.when(owner)
    def _():
        t01a, t01b = pa[0, 0, 0, kz], pa[0, 0, 1, kz]
        ba, bb = pb[0, 0, 0, kz, :HA], pb[0, 0, 1, kz, :HA]
        d0, d1 = pb[0, 0, 0, kz, HA : HA + 1], pb[0, 0, 1, kz, HA : HA + 1]
        def arrive3(d, total):
            remote(got3.at[d], got3.at[d], l3_ss.at[0], l3_rs.at[d], sibling).wait_recv()
            parts, rows = decode(got3.at[d], 4096)
            return tuple(a + b for a, b in zip(total, (*parts, rows[2], rows[3])))

        t01a, t01b, ba, bb, d0, d1 = lax.fori_loop(1, NZ, arrive3, (t01a, t01b, ba, bb, d0, d1))
        scale = 1.0 / TOTAL
        t01 = jnp.concatenate([t01a, t01b], axis=0) * scale
        both = jnp.concatenate([ba, bb], axis=0) * scale
        damp = damping[slot_block[0, dp]]
        d0 = d0 * scale + damp
        d1 = d1 * scale + damp
        flip = both.T
        t00 = jnp.where(row < col, both, jnp.where(row > col, flip, d0))
        t11 = jnp.where(row > col, both, jnp.where(row < col, flip, d1))
        mat = jnp.concatenate(
            [jnp.concatenate([t00, t01], axis=1), jnp.concatenate([t01.T, t11], axis=1)], axis=0
        )
        alpha = 1.0 / jnp.max(jnp.sum(jnp.abs(mat), axis=0, keepdims=True), axis=1, keepdims=True)

        def times(v):
            return jnp.dot(v, mat, precision=lax.Precision.HIGHEST, preferred_element_type=F32)

        def first(v):
            return 2.0 * alpha * v - alpha * alpha * times(v)

        def second(v):
            p = first(v)
            return 2.0 * p - first(times(p))

        v = second(slab_t[...])
        result = 2.0 * v - second(times(v))
        gathered[c, xy, 0] = result.astype(BF16)
        for d in (1, 7, 4, 3, 5, 2, 6):
            ag1(d).start()

    def along(j, e, d):
        even = j % 2 == 0
        return ((x + jnp.where(even, d, e)) % NX) * NY + (y + jnp.where(even, e, d)) % NY

    def whole(j, q, s, r, dev):
        return remote(gathered.at[c, q, j], gathered.at[c, q, j], s, r, dev)

    def ag2(j, d):
        return whole(j, xy, ag2_s.at[j, d], ag_r.at[j, xy], (along(j, d, 0) * NZ + z, c))

    def ag3(j, e, d):
        q = along(j, e, 0)
        return whole(j, q, ag3_s.at[j, e, d], ag_r.at[j, q], (along(j, 0, d) * NZ + z, c))

    def landed(j, q):
        whole(j, q, ag2_s.at[0, 0], ag_r.at[j, q], sibling).wait_recv()

    def forward(cc, j, q):
        return remote(gathered.at[cc, q, j], gathered.at[cc, q, j], fw_s.at[j, q], fw_r.at[j, q], sibling)

    def pass1(j, carry):
        @pl.when(jnp.logical_or(j > 0, jnp.logical_not(owner)))
        def _():
            whole(j, xy, ag1_s.at[0], ag1_r.at[j], sibling).wait_recv()

        for d in (2, 1, 3):
            ag2(j, d).start()
        for d in (2, 1, 3):
            ag3(j, 0, d).start()
        forward(c, j, xy).start()
        return carry

    def pass2(i, carry):
        j, e = i // 3, 2 * (i % 3) + 1 - 3 * ((i % 3) // 2)
        q = along(j, e, 0)
        landed(j, q)
        for d in (2, 1, 3):
            ag3(j, e, d).start()
        forward(c, j, q).start()
        return carry

    def pass3(i, carry):
        j, e = i // 4, i % 4
        for d in (1, 3, 2):
            q = along(j, e, d)
            landed(j, q)
            forward(c, j, q).start()
        return carry

    lax.fori_loop(0, NK, pass1, 0)
    lax.fori_loop(0, 3 * NK, pass2, 0)
    lax.fori_loop(0, 4 * NK, pass3, 0)

    def sent_exchange(g, carry):
        remote(xs.at[g], xr.at[g], ex_s.at[g], ex_r.at[g], sibling).wait_send()
        return carry

    lax.fori_loop(0, 16, sent_exchange, 0)

    @pl.when(c == 1)
    def _():
        each1((0, 1), lambda copy: copy.wait_send())

    each1((2,), lambda copy: copy.wait_send())
    for part in (0, 1):
        for d in (1, 2, 3):
            for pair in (0, 1):
                level2(part, d, pair).wait_send()
    for k in range(NK):
        @pl.when(2 * k + c != z)
        def _():
            level3(k).wait_send()

    @pl.when(owner)
    def _():
        for d in range(1, NZ):
            ag1(d).wait_send()

    def sent_gather(j, carry):
        for d in (1, 2, 3):
            ag2(j, d).wait_send()
            for e in range(4):
                ag3(j, e, d).wait_send()
        return carry

    lax.fori_loop(0, NK, sent_gather, 0)

    def sent_forward(q, carry):
        for j in range(NK):
            forward(c, j, q).wait_send()
            forward(1 - c, j, q).wait_recv()
        return carry

    lax.fori_loop(0, 16, sent_forward, 0)


def permute_kernel(owner_of, gathered, out, sem):
    here = lax.axis_index("dp") % NZ
    nearest = [lax.shift_right_logical(here - plane + NZ, 1) & (NK - 1) for plane in (0, 1)]

    def one(b, carry):
        o = owner_of[b]
        q, plane = lax.shift_right_logical(o, 3), o & 1
        away = (lax.shift_right_logical(o, 1) - jnp.where(plane == 0, *nearest)) & (NK - 1)
        j = away ^ lax.shift_right_logical(away, 1)
        pltpu.make_async_copy(
            gathered.at[plane, q, j], out.at[:, pl.ds(pl.multiple_of(b * B, B), B)], sem
        ).start()
        return carry

    lax.fori_loop(0, OWNERS, one, 0, unroll=8)
    pltpu.make_async_copy(out, out, sem).wait()


def shards(features, grad_slab, damping, owner_of):
    vmem = pl.BlockSpec(memory_space=pltpu.VMEM)
    smem = pl.BlockSpec(memory_space=pltpu.SMEM)
    dma = pltpu.SemaphoreType.DMA
    gathered = pl.pallas_call(
        reduce_kernel,
        out_shape=pltpu.VMEM((2, NX * NY, NK, COLS, B), BF16),
        in_specs=[vmem] + [pl.BlockSpec(memory_space=pl.ANY)] * 3,
        out_specs=vmem,
        scratch_shapes=[
            pltpu.SMEM((1, OWNERS), jnp.int32),
            pltpu.SMEM((OWNERS,), F32),
            pltpu.VMEM((COLS, B), F32),
            pltpu.VMEM((1, OWNERS), jnp.int32),
            pltpu.VMEM((OWNERS, ROWS, B), BF16),
            pltpu.VMEM((16, NK, ROWS, B), BF16),
            pltpu.VMEM((16, NK, ROWS, B), BF16),
            pltpu.VMEM((4, 4, 2, NK, HA, H), F32),
            pltpu.VMEM((4, 4, 2, NK, HB, H), F32),
            pltpu.VMEM((3, 2, 2, 4, CODED, H), jnp.int16),
            pltpu.VMEM((3, 2, 2, 4, CODED, H), jnp.int16),
            pltpu.VMEM((2, 4, 2, CODED, H), jnp.int16),
            pltpu.VMEM((2, 4, 2, CODED, H), jnp.int16),
            pltpu.VMEM((NK, CODED, H), jnp.int16),
            pltpu.VMEM((NZ, CODED, H), jnp.int16),
            pltpu.SemaphoreType.REGULAR, dma((3,)), dma,
            dma((16,)), dma((16,)),
            dma((3, 2, 2, 4)), dma((3, 2, 2, 4)),
            dma((2, 4, 2)), dma((2, 4, 2)),
            dma((NK,)), dma((NZ,)),
            dma((NZ,)), dma((NK,)),
            dma((NK, 4)), dma((NK, 4, 4)), dma((NK, 16)),
            dma((NK, 16)), dma((NK, 16)),
        ],
        compiler_params=pltpu.CompilerParams(
            collective_id=0, has_side_effects=True, vmem_limit_bytes=58 * 1024 * 1024
        ),
    )(owner_of.reshape(1, OWNERS), damping, features, grad_slab.T)
    out = pl.pallas_call(
        permute_kernel,
        out_shape=jax.ShapeDtypeStruct((COLS, OWNERS * B), BF16),
        in_specs=[smem, vmem],
        out_specs=pl.BlockSpec(memory_space=pl.ANY),
        scratch_shapes=[dma],
        compiler_params=pltpu.CompilerParams(vmem_limit_bytes=32 * 1024 * 1024),
    )(owner_of, gathered)
    return out.T


def solution(mesh):
    return jax.shard_map(
        shards,
        mesh=mesh,
        in_specs=(P(("dp", "group"), None), P("dp", None), P(), P()),
        out_specs=P(),
        check_vma=False,
    )
```

```python
import jax
import jax.numpy as jnp
from jax import lax
from jax.experimental import pallas as pl
from jax.experimental.pallas import tpu as pltpu
from jax.sharding import PartitionSpec as P

B = 256
H = B // 2
COLS = 64
TOTAL = 32768
NX, NY, NZ = 4, 4, 8
NK = NZ // 2
OWNERS = NX * NY * NZ
ROWS = 128
AHEAD = 8
HA = 64
HB = 72
CODED = 4 * HA + 16
F32 = jnp.float32
BF16 = jnp.bfloat16
MESH = pl.DeviceIdType.MESH


def order(i):
    return jnp.where(i == 0, 2, jnp.where(i == 3, 0, 2 * i - 1))


def pick(g):
    r = jnp.maximum(g - 7, 0)
    even = g % 2 == 0
    dx = jnp.where(g < 7, jnp.where(even, 2, order((g + 1) // 2)), order(1 + r // 3))
    dy = jnp.where(g < 7, jnp.where(even, order(g // 2), 2), order(1 + r % 3))
    return dx, dy


def rank(z, c, k):
    away = (k - (z - c + NZ) // 2 % NK + NK) % NK
    return away + away // 2 - 2 * (away // 3)


def dp_index(x, y, z):
    return (x * NY + y) * NZ + z


def encode(ref, parts, diagonals, tokens):
    unit = tokens // 512
    line = lax.broadcasted_iota(jnp.int32, (16, H), 0)
    extra = jnp.zeros((16, H), F32)
    for i, v in enumerate(parts):
        top = jnp.max(jnp.abs(v), axis=0, keepdims=True)
        units = jnp.maximum(jnp.ceil(top * (1.0 / unit)), 1.0)
        coded = jnp.round(v * ((32767.0 / unit) / units))
        ref[HA * i : HA * (i + 1)] = coded.astype(jnp.int32).astype(jnp.int16)
        extra = jnp.where(line == i, units, extra)
    for i, d in diagonals.items():
        scaled = d * (32767.0 / (36.0 * tokens))
        high = jnp.floor(scaled)
        low = jnp.round((scaled - high) * 32767.0)
        extra = jnp.where(line == 4 + i, high, jnp.where(line == 8 + i, low, extra))
    ref[4 * HA :] = extra.astype(jnp.int32).astype(jnp.int16)


def decode(ref, tokens):
    unit = tokens // 512
    extra = ref[4 * HA :].astype(jnp.int32).astype(F32)
    parts = []
    for i in range(4):
        v = ref[HA * i : HA * (i + 1)].astype(jnp.int32).astype(F32)
        parts.append(v * (extra[i : i + 1] * (unit / 32767.0)))
    rows = (extra[4:8] + extra[8:12] * (1.0 / 32767.0)) * (36.0 * tokens / 32767.0)
    return parts, [rows[i : i + 1] for i in range(4)]


def thirds(v):
    high = v.astype(BF16)
    rest = v - high.astype(F32)
    middle = rest.astype(BF16)
    return high, middle, (rest - middle.astype(F32)).astype(BF16)


def reduce_kernel(
    owner_of, damping_in, features, slab_in, gathered,
    slot_block, damping, slab_t, table, feat, xs, xr, pa, pb, sent1, got1, sent2, got2, sent3, got3,
    turn, small_sem, feat_sem, ex_s, ex_r, l1_s, l1_r, l2_s, l2_r, l3_ss, l3_rs,
    ag1_s, ag1_r, ag_s, ag_r, fw_s, fw_r,
):
    dp = lax.axis_index("dp")
    c = lax.axis_index("group")
    x = dp // (NY * NZ)
    y = (dp // NZ) % NY
    z = dp % NZ

    def at(xx, yy, zz, cc):
        return (dp_index(xx, yy, zz), cc)

    sibling = (dp, 1 - c)
    xnb = [at((x + d) % NX, y, z, c) for d in range(NX)]
    ynb = [at(x, (y + d) % NY, z, c) for d in range(NY)]
    znb = [at(x, y, (z + d) % NZ, c) for d in range(NZ)]

    barrier = pltpu.get_barrier_semaphore()
    peers = [sibling] + xnb[1:] + ynb[1:] + znb[1:]
    for peer in peers:
        pl.semaphore_signal(barrier, inc=1, device_id=peer, device_id_type=MESH)
    small = [
        pltpu.make_async_copy(a, b, small_sem.at[i])
        for i, (a, b) in enumerate(((damping_in, damping), (slab_in, slab_t)))
    ]
    for copy in small:
        copy.start()

    def load(b, carry):
        pltpu.make_async_copy(features.at[:, pl.ds(pl.multiple_of(b * B, B), B)], feat.at[b], feat_sem).start()
        return carry

    lax.fori_loop(0, OWNERS, load, 0)

    def remote(src, dst, s, r, dev):
        return pltpu.make_async_remote_copy(
            src_ref=src, dst_ref=dst, send_sem=s, recv_sem=r, device_id=dev, device_id_type=MESH
        )

    row = lax.broadcasted_iota(jnp.int32, (H, H), 0)
    col = lax.broadcasted_iota(jnp.int32, (H, H), 1)
    owners = jnp.broadcast_to(owner_of[...].astype(F32), (OWNERS, OWNERS)).T
    held = jnp.where(owners == col.astype(F32), row, 0)
    table[...] = jnp.minimum(jnp.sum(held, axis=0, keepdims=True), OWNERS - 1)
    copy = pltpu.make_async_copy(table, slot_block, small_sem.at[2])
    copy.start()
    copy.wait()
    pltpu.make_async_copy(feat, feat, feat_sem).wait()
    for copy in small:
        copy.wait()

    def slot_of(dx, dy, k, cc):
        return dp_index((x + dx) % NX, (y + dy) % NY, 2 * k + cc)

    def block_of(dx, dy, k, cc):
        return feat[slot_block[0, slot_of(dx, dy, k, cc)]]

    def stage(g, carry):
        dx, dy = pick(g)
        for k in range(NK):
            xs[g, k] = block_of(dx, dy, k, 1 - c)
        return carry

    lax.fori_loop(0, AHEAD, stage, 0)
    pl.semaphore_wait(barrier, len(peers))

    def exchange(g, carry):
        remote(xs.at[g], xr.at[g], ex_s.at[g], ex_r.at[g], sibling).start()
        return carry

    lax.fori_loop(0, AHEAD, exchange, 0)

    def level1(kind, axis, way, t):
        dev = (xnb, ynb)[axis][1 if way == 0 else 3]
        return remote(
            sent1.at[kind, axis, way, t], got1.at[kind, axis, way, t],
            l1_s.at[kind, axis, way, t], l1_r.at[kind, axis, way, t], dev,
        )

    def place(part, d, t):
        return pa.at[d, t] if part == 0 else pb.at[t, d]

    def pieces(ref, part, half):
        parts = [ref[half, k, :HA] for k in range(NK)]
        return parts, ({k: ref[half, k, HA : HA + 1] for k in range(NK)} if part == 1 else {})

    def send1(kind, part, d, half, way, t):
        parts, diagonals = pieces(place(part, d, t), part, half)
        encode(sent1.at[kind, part, way, t], parts, diagonals, 512)

        @pl.when(c == 0)
        def _():
            level1(kind, part, way, t).start()

    def group(g, carry):
        dx, dy = pick(g)

        @pl.when(g + AHEAD < 16)
        def _():
            stage(g + AHEAD, 0)
            exchange(g + AHEAD, 0)

        remote(xs.at[g], xr.at[g], ex_s.at[g], ex_r.at[g], sibling).wait_recv()

        for k in range(NK):
            own = block_of(dx, dy, k, c)
            f = jnp.concatenate([own, xr[g, k]], axis=0)
            t = lax.dot_general(f, f, (((0,), (0,)), ((), ())), preferred_element_type=F32)
            t00, t01, t11 = t[:H, :H], t[:H, H:], t[H:, H:]
            pa[dx, dy, 0, k] = t01[:HA]
            pa[dx, dy, 1, k] = t01[HA:]
            on = row == col
            both = jnp.where(row < col, t00, jnp.where(on, 0.0, t11))
            d0 = jnp.sum(jnp.where(on, t00, 0.0), axis=0, keepdims=True)
            d1 = jnp.sum(jnp.where(on, t11, 0.0), axis=0, keepdims=True)
            pb[dx, dy, 0, k, :HA] = both[:HA]
            pb[dx, dy, 0, k, HA:] = jnp.broadcast_to(d0, (HB - HA, H))
            pb[dx, dy, 1, k, :HA] = both[HA:]
            pb[dx, dy, 1, k, HA:] = jnp.broadcast_to(d1, (HB - HA, H))

        for part, d, t in ((0, dx, dy), (1, dy, dx)):
            @pl.when(d == 2)
            def _():
                send1(0, part, 2, 0, 0, t)
                send1(0, part, 2, 1, 1, t)

            @pl.when(d == 1)
            def _():
                send1(1, part, 1, 1, 0, t)

            @pl.when(d == 3)
            def _():
                send1(1, part, 3, 0, 1, t)
        return carry

    lax.fori_loop(0, 16, group, 0)

    def each1(kinds, action):
        def step(i, carry):
            for kind in kinds:
                for part in (0, 1):
                    for way in (0, 1):
                        action(level1(kind, part, way, order(i)))
            return carry

        lax.fori_loop(0, 4, step, 0)

    @pl.when(c == 1)
    def _():
        pl.semaphore_wait(turn, 1)
        each1((0,), lambda copy: copy.start())
        each1((1,), lambda copy: copy.start())

    def pass_on(i, carry):
        t = order(i)
        for part in (0, 1):
            for way, d in ((0, 1), (1, 3)):
                level1(0, part, way, t).wait_recv()
                parts, rows = decode(got1.at[0, part, way, t], 512)
                own, diagonals = pieces(place(part, d, t), part, way)
                parts = [a + b for a, b in zip(own, parts)]
                diagonals = {k: diagonals[k] + rows[k] for k in diagonals}
                encode(sent1.at[2, part, way, t], parts, diagonals, 512)
                level1(2, part, way, t).start()
        return carry

    lax.fori_loop(0, 4, pass_on, 0)

    def add_coded(ref, part, half, coded):
        for message in coded:
            parts, rows = decode(message, 512)
            for k in range(NK):
                ref[half, k, :HA] = ref[half, k, :HA] + parts[k]
                if part == 1:
                    ref[half, k, HA:] = ref[half, k, HA:] + rows[k]

    def level2(part, d, pair):
        dev = at(x, (y + d) % NY, z, c) if part == 0 else at((x + d) % NX, y, z, c)
        return remote(
            sent2.at[part, d, pair], got2.at[part, d, pair], l2_s.at[part, d, pair], l2_r.at[part, d, pair], dev
        )

    halves = [(half, n) for half in (0, 1) for n in (0, 1)]

    def far(pair, n):
        return ((z - c + NZ) // 2 + ((2, 3), (1, 0))[pair][n]) % NK

    def send2(part, t, pair):
        ref = place(part, 0, t)
        parts = [ref[half, far(pair, n), :HA] for half, n in halves]
        diagonals = {2 * half + n: ref[half, far(pair, n), HA : HA + 1] for half, n in halves} if part == 1 else {}
        encode(sent2.at[part, t, pair], parts, diagonals, 1024)
        level2(part, t, pair).start()

    def finish1(i, carry):
        t = order(i)
        for part in (0, 1):
            for way in (0, 1):
                level1(1, part, way, t).wait_recv()
                level1(2, part, way, t).wait_recv()
            ref = place(part, 0, t)
            for half in (0, 1):
                add_coded(ref, part, half, (got1.at[2, part, half, t], got1.at[1, part, 1 - half, t]))

            @pl.when(t != 0)
            def _():
                send2(part, t, 0)
        return carry

    lax.fori_loop(0, 4, finish1, 0)

    @pl.when(c == 0)
    def _():
        each1((0, 1), lambda copy: copy.wait_send())
        pl.semaphore_signal(turn, inc=1, device_id=sibling, device_id_type=MESH)

    def second_pair(i, carry):
        for part in (0, 1):
            send2(part, order(i), 1)
        return carry

    lax.fori_loop(0, 3, second_pair, 0)

    def level3(k):
        d = (2 * k + c - z + NZ) % NZ
        return remote(sent3.at[k], got3.at[d], l3_ss.at[k], l3_rs.at[d], at(x, y, 2 * k + c, c))

    def send3(k):
        @pl.when(2 * k + c != z)
        def _():
            parts = [pa[0, 0, 0, k], pa[0, 0, 1, k], pb[0, 0, 0, k, :HA], pb[0, 0, 1, k, :HA]]
            diagonals = {2: pb[0, 0, 0, k, HA : HA + 1], 3: pb[0, 0, 1, k, HA : HA + 1]}
            encode(sent3.at[k], parts, diagonals, 4096)
            level3(k).start()

    for pair in (0, 1):
        for part in (0, 1):
            ref = place(part, 0, 0)
            for d in (1, 3, 2):
                level2(part, d, pair).wait_recv()
                parts, rows = decode(got2.at[part, d, pair], 1024)
                for half, n in halves:
                    k = far(pair, n)
                    ref[half, k, :HA] = ref[half, k, :HA] + parts[2 * half + n]
                    if part == 1:
                        ref[half, k, HA:] = ref[half, k, HA:] + rows[2 * half + n]
        for n in (0, 1):
            send3(far(pair, n))

    owner = z % 2 == c
    xy = x * NY + y
    kz = z // 2

    def ag1(d):
        j = rank((z + d) % NZ, c, kz)
        return remote(gathered.at[c, xy, 0], gathered.at[c, xy, j], ag1_s.at[d], ag1_r.at[j], znb[d])

    @pl.when(owner)
    def _():
        t01a, t01b = pa[0, 0, 0, kz], pa[0, 0, 1, kz]
        ba, bb = pb[0, 0, 0, kz, :HA], pb[0, 0, 1, kz, :HA]
        d0, d1 = pb[0, 0, 0, kz, HA : HA + 1], pb[0, 0, 1, kz, HA : HA + 1]
        def arrive3(d, total):
            remote(got3.at[d], got3.at[d], l3_ss.at[0], l3_rs.at[d], sibling).wait_recv()
            parts, rows = decode(got3.at[d], 4096)
            return tuple(a + b for a, b in zip(total, (*parts, rows[2], rows[3])))

        t01a, t01b, ba, bb, d0, d1 = lax.fori_loop(1, NZ, arrive3, (t01a, t01b, ba, bb, d0, d1))
        scale = 1.0 / TOTAL
        t01 = jnp.concatenate([t01a, t01b], axis=0) * scale
        both = jnp.concatenate([ba, bb], axis=0) * scale
        damp = damping[slot_block[0, dp]]
        d0 = d0 * scale + damp
        d1 = d1 * scale + damp
        flip = both.T
        t00 = jnp.where(row < col, both, jnp.where(row > col, flip, d0))
        t11 = jnp.where(row > col, both, jnp.where(row < col, flip, d1))
        mat = jnp.concatenate(
            [jnp.concatenate([t00, t01], axis=1), jnp.concatenate([t01.T, t11], axis=1)], axis=0
        )
        alpha = 1.0 / jnp.max(jnp.sum(jnp.abs(mat), axis=0, keepdims=True), axis=1, keepdims=True)

        m1, m2, m3 = thirds(mat)

        def times(v):
            v1, v2, v3 = thirds(v)
            a = jnp.dot(jnp.concatenate([v1, v2, v3], axis=0), m1, preferred_element_type=F32)
            b = jnp.dot(jnp.concatenate([v1, v2], axis=0), m2, preferred_element_type=F32)
            e = jnp.dot(v1, m3, preferred_element_type=F32)
            small = a[2 * COLS :] + b[COLS:] + e
            return a[:COLS] + ((a[COLS : 2 * COLS] + b[:COLS]) + small)

        def first(v):
            return 2.0 * alpha * v - alpha * alpha * times(v)

        def second(v):
            p = first(v)
            return 2.0 * p - first(times(p))

        v = second(slab_t[...])
        result = 2.0 * v - second(times(v))
        gathered[c, xy, 0] = result.astype(BF16)
        for d in (1, 7, 4, 3, 5, 2, 6):
            ag1(d).start()

    def sent_exchange(g, carry):
        remote(xs.at[g], xr.at[g], ex_s.at[g], ex_r.at[g], sibling).wait_send()
        return carry

    lax.fori_loop(0, 16, sent_exchange, 0)

    @pl.when(c == 1)
    def _():
        each1((0, 1), lambda copy: copy.wait_send())

    each1((2,), lambda copy: copy.wait_send())
    for part in (0, 1):
        for d in (1, 2, 3):
            for pair in (0, 1):
                level2(part, d, pair).wait_send()
    for k in range(NK):
        @pl.when(2 * k + c != z)
        def _():
            level3(k).wait_send()

    def along(j, e, d):
        even = j % 2 == 0
        return ((x + jnp.where(even, d, e)) % NX) * NY + (y + jnp.where(even, e, d)) % NY

    def whole(j, q, s, r, dev):
        return remote(gathered.at[c, q, j], gathered.at[c, q, j], s, r, dev)

    def ag2(j, d):
        return whole(j, xy, ag_s, ag_r.at[j, xy], (along(j, d, 0) * NZ + z, c))

    def ag3(j, e, d):
        q = along(j, e, 0)
        return whole(j, q, ag_s, ag_r.at[j, q], (along(j, 0, d) * NZ + z, c))

    def landed(j, q):
        whole(j, q, ag_s, ag_r.at[j, q], sibling).wait_recv()

    def forward(cc, j, q):
        return remote(gathered.at[cc, q, j], gathered.at[cc, q, j], fw_s, fw_r, sibling)

    def pass1(j, carry):
        @pl.when(jnp.logical_or(j > 0, jnp.logical_not(owner)))
        def _():
            whole(j, xy, ag1_s.at[0], ag1_r.at[j], sibling).wait_recv()

        for d in (2, 1, 3):
            ag2(j, d).start()
        for d in (2, 1, 3):
            ag3(j, 0, d).start()
        forward(c, j, xy).start()
        return carry

    def pass2(i, carry):
        j, e = i // 3, 2 * (i % 3) + 1 - 3 * ((i % 3) // 2)
        q = along(j, e, 0)
        landed(j, q)
        for d in (2, 1, 3):
            ag3(j, e, d).start()
        forward(c, j, q).start()
        return carry

    def pass3(i, carry):
        j, e = i // 4, i % 4
        for d in (1, 3, 2):
            q = along(j, e, d)
            landed(j, q)
            forward(c, j, q).start()
        return carry

    lax.fori_loop(0, NK, pass1, 0)
    lax.fori_loop(0, 3 * NK, pass2, 0)
    lax.fori_loop(0, 4 * NK, pass3, 0)

    @pl.when(owner)
    def _():
        for d in range(1, NZ):
            ag1(d).wait_send()

    most = gathered.at[c, pl.ds(0, 15)]
    remote(most, most, ag_s, ag_r.at[0, 0], sibling).wait_send()
    remote(gathered.at[c], gathered.at[c], fw_s, fw_r, sibling).wait_send()
    remote(gathered.at[1 - c], gathered.at[1 - c], fw_s, fw_r, sibling).wait_recv()


def permute_kernel(owner_of, gathered, out, sem):
    here = lax.axis_index("dp") % NZ
    nearest = [lax.shift_right_logical(here - plane + NZ, 1) & (NK - 1) for plane in (0, 1)]

    def one(b, carry):
        o = owner_of[b]
        q, plane = lax.shift_right_logical(o, 3), o & 1
        away = (lax.shift_right_logical(o, 1) - jnp.where(plane == 0, *nearest)) & (NK - 1)
        j = away ^ lax.shift_right_logical(away, 1)
        pltpu.make_async_copy(
            gathered.at[plane, q, j], out.at[:, pl.ds(pl.multiple_of(b * B, B), B)], sem
        ).start()
        return carry

    lax.fori_loop(0, OWNERS, one, 0, unroll=8)
    pltpu.make_async_copy(out, out, sem).wait()


def shards(features, grad_slab, damping, owner_of):
    vmem = pl.BlockSpec(memory_space=pltpu.VMEM)
    smem = pl.BlockSpec(memory_space=pltpu.SMEM)
    dma = pltpu.SemaphoreType.DMA
    gathered = pl.pallas_call(
        reduce_kernel,
        out_shape=pltpu.VMEM((2, NX * NY, NK, COLS, B), BF16),
        in_specs=[vmem] + [pl.BlockSpec(memory_space=pl.ANY)] * 3,
        out_specs=vmem,
        scratch_shapes=[
            pltpu.SMEM((1, OWNERS), jnp.int32),
            pltpu.SMEM((OWNERS,), F32),
            pltpu.VMEM((COLS, B), F32),
            pltpu.VMEM((1, OWNERS), jnp.int32),
            pltpu.VMEM((OWNERS, ROWS, B), BF16),
            pltpu.VMEM((16, NK, ROWS, B), BF16),
            pltpu.VMEM((16, NK, ROWS, B), BF16),
            pltpu.VMEM((4, 4, 2, NK, HA, H), F32),
            pltpu.VMEM((4, 4, 2, NK, HB, H), F32),
            pltpu.VMEM((3, 2, 2, 4, CODED, H), jnp.int16),
            pltpu.VMEM((3, 2, 2, 4, CODED, H), jnp.int16),
            pltpu.VMEM((2, 4, 2, CODED, H), jnp.int16),
            pltpu.VMEM((2, 4, 2, CODED, H), jnp.int16),
            pltpu.VMEM((NK, CODED, H), jnp.int16),
            pltpu.VMEM((NZ, CODED, H), jnp.int16),
            pltpu.SemaphoreType.REGULAR, dma((3,)), dma,
            dma((16,)), dma((16,)),
            dma((3, 2, 2, 4)), dma((3, 2, 2, 4)),
            dma((2, 4, 2)), dma((2, 4, 2)),
            dma((NK,)), dma((NZ,)),
            dma((NZ,)), dma((NK,)),
            dma, dma((NK, 16)), dma, dma,
        ],
        compiler_params=pltpu.CompilerParams(
            collective_id=0, has_side_effects=True, vmem_limit_bytes=58 * 1024 * 1024
        ),
    )(owner_of.reshape(1, OWNERS), damping, features, grad_slab.T)
    out = pl.pallas_call(
        permute_kernel,
        out_shape=jax.ShapeDtypeStruct((COLS, OWNERS * B), BF16),
        in_specs=[smem, vmem],
        out_specs=pl.BlockSpec(memory_space=pl.ANY),
        scratch_shapes=[dma],
        compiler_params=pltpu.CompilerParams(vmem_limit_bytes=32 * 1024 * 1024),
    )(owner_of, gathered)
    return out.T


def solution(mesh):
    return jax.shard_map(
        shards,
        mesh=mesh,
        in_specs=(P(("dp", "group"), None), P("dp", None), P(), P()),
        out_specs=P(),
        check_vma=False,
    )
```

```python
import jax
import jax.numpy as jnp
from jax import lax
from jax.experimental import pallas as pl
from jax.experimental.pallas import tpu as pltpu
from jax.sharding import PartitionSpec as P

B = 256
H = B // 2
COLS = 64
TOTAL = 32768
NX, NY, NZ = 4, 4, 8
NK = NZ // 2
OWNERS = NX * NY * NZ
ROWS = 128
AHEAD = 8
HA = 64
HB = 72
CODED = 4 * HA + 16
F32 = jnp.float32
BF16 = jnp.bfloat16
MESH = pl.DeviceIdType.MESH


def order(i):
    return jnp.where(i == 0, 2, jnp.where(i == 3, 0, 2 * i - 1))


def pick(g):
    r = jnp.maximum(g - 7, 0)
    even = g % 2 == 0
    dx = jnp.where(g < 7, jnp.where(even, 2, order((g + 1) // 2)), order(1 + r // 3))
    dy = jnp.where(g < 7, jnp.where(even, order(g // 2), 2), order(1 + r % 3))
    return dx, dy


def rank(z, c, k):
    away = (k - (z - c + NZ) // 2 % NK + NK) % NK
    return away + away // 2 - 2 * (away // 3)


def dp_index(x, y, z):
    return (x * NY + y) * NZ + z


def encode(ref, parts, diagonals, tokens):
    unit = tokens // 512
    line = lax.broadcasted_iota(jnp.int32, (16, H), 0)
    extra = jnp.zeros((16, H), F32)
    for i, v in enumerate(parts):
        top = jnp.max(jnp.abs(v), axis=0, keepdims=True)
        units = jnp.maximum(jnp.ceil(top * (1.0 / unit)), 1.0)
        coded = jnp.round(v * ((32767.0 / unit) / units))
        ref[HA * i : HA * (i + 1)] = coded.astype(jnp.int32).astype(jnp.int16)
        extra = jnp.where(line == i, units, extra)
    for i, d in diagonals.items():
        scaled = d * (32767.0 / (36.0 * tokens))
        high = jnp.floor(scaled)
        low = jnp.round((scaled - high) * 32767.0)
        extra = jnp.where(line == 4 + i, high, jnp.where(line == 8 + i, low, extra))
    ref[4 * HA :] = extra.astype(jnp.int32).astype(jnp.int16)


def decode(ref, tokens):
    unit = tokens // 512
    extra = ref[4 * HA :].astype(jnp.int32).astype(F32)
    parts = []
    for i in range(4):
        v = ref[HA * i : HA * (i + 1)].astype(jnp.int32).astype(F32)
        parts.append(v * (extra[i : i + 1] * (unit / 32767.0)))
    rows = (extra[4:8] + extra[8:12] * (1.0 / 32767.0)) * (36.0 * tokens / 32767.0)
    return parts, [rows[i : i + 1] for i in range(4)]


def thirds(v):
    high = v.astype(BF16)
    rest = v - high.astype(F32)
    middle = rest.astype(BF16)
    return high, middle, (rest - middle.astype(F32)).astype(BF16)


def reduce_kernel(
    owner_of, damping_in, features, slab_in, gathered,
    slot_block, damping, slab_t, table, feat, xs, xr, pa, pb, sent1, got1, sent2, got2, sent3, got3,
    turn, small_sem, feat_sem, ex_s, ex_r, l1_s, l1_r, l2_s, l2_r, l3_ss, l3_rs,
    ag1_s, ag1_r, ag_s, ag_r, fw_s, fw_r,
):
    dp = lax.axis_index("dp")
    c = lax.axis_index("group")
    x = dp // (NY * NZ)
    y = (dp // NZ) % NY
    z = dp % NZ

    def at(xx, yy, zz, cc):
        return (dp_index(xx, yy, zz), cc)

    sibling = (dp, 1 - c)
    xnb = [at((x + d) % NX, y, z, c) for d in range(NX)]
    ynb = [at(x, (y + d) % NY, z, c) for d in range(NY)]
    znb = [at(x, y, (z + d) % NZ, c) for d in range(NZ)]

    barrier = pltpu.get_barrier_semaphore()
    peers = [sibling] + xnb[1:] + ynb[1:] + znb[1:]
    for peer in peers:
        pl.semaphore_signal(barrier, inc=1, device_id=peer, device_id_type=MESH)
    small = [
        pltpu.make_async_copy(a, b, small_sem.at[i])
        for i, (a, b) in enumerate(((damping_in, damping), (slab_in, slab_t)))
    ]
    for copy in small:
        copy.start()

    def load(b, carry):
        pltpu.make_async_copy(features.at[:, pl.ds(pl.multiple_of(b * B, B), B)], feat.at[b], feat_sem).start()
        return carry

    lax.fori_loop(0, OWNERS, load, 0)

    def remote(src, dst, s, r, dev):
        return pltpu.make_async_remote_copy(
            src_ref=src, dst_ref=dst, send_sem=s, recv_sem=r, device_id=dev, device_id_type=MESH
        )

    row = lax.broadcasted_iota(jnp.int32, (H, H), 0)
    col = lax.broadcasted_iota(jnp.int32, (H, H), 1)
    owners = jnp.broadcast_to(owner_of[...].astype(F32), (OWNERS, OWNERS)).T
    held = jnp.where(owners == col.astype(F32), row, 0)
    table[...] = jnp.minimum(jnp.sum(held, axis=0, keepdims=True), OWNERS - 1)
    copy = pltpu.make_async_copy(table, slot_block, small_sem.at[2])
    copy.start()
    copy.wait()
    pltpu.make_async_copy(feat, feat, feat_sem).wait()
    for copy in small:
        copy.wait()

    def slot_of(dx, dy, k, cc):
        return dp_index((x + dx) % NX, (y + dy) % NY, 2 * k + cc)

    def block_of(dx, dy, k, cc):
        return feat[slot_block[0, slot_of(dx, dy, k, cc)]]

    def stage(g, carry):
        dx, dy = pick(g)
        for k in range(NK):
            xs[g, k] = block_of(dx, dy, k, 1 - c)
        return carry

    lax.fori_loop(0, AHEAD, stage, 0)
    pl.semaphore_wait(barrier, len(peers))

    def exchange(g, carry):
        remote(xs.at[g], xr.at[g], ex_s.at[g], ex_r.at[g], sibling).start()
        return carry

    lax.fori_loop(0, AHEAD, exchange, 0)

    def level1(kind, axis, way, t):
        dev = (xnb, ynb)[axis][1 if way == 0 else 3]
        return remote(
            sent1.at[kind, axis, way, t], got1.at[kind, axis, way, t],
            l1_s.at[kind, axis, way, t], l1_r.at[kind, axis, way, t], dev,
        )

    def place(part, d, t):
        return pa.at[d, t] if part == 0 else pb.at[t, d]

    def pieces(ref, part, half):
        parts = [ref[half, k, :HA] for k in range(NK)]
        return parts, ({k: ref[half, k, HA : HA + 1] for k in range(NK)} if part == 1 else {})

    def send1(kind, part, d, half, way, t):
        parts, diagonals = pieces(place(part, d, t), part, half)
        encode(sent1.at[kind, part, way, t], parts, diagonals, 512)

        @pl.when(c == 0)
        def _():
            level1(kind, part, way, t).start()

    def group(g, carry):
        dx, dy = pick(g)

        @pl.when(g + AHEAD < 16)
        def _():
            stage(g + AHEAD, 0)
            exchange(g + AHEAD, 0)

        remote(xs.at[g], xr.at[g], ex_s.at[g], ex_r.at[g], sibling).wait_recv()

        for k in range(NK):
            own = block_of(dx, dy, k, c)
            f = jnp.concatenate([own, xr[g, k]], axis=0)
            t = lax.dot_general(f, f, (((0,), (0,)), ((), ())), preferred_element_type=F32)
            t00, t01, t11 = t[:H, :H], t[:H, H:], t[H:, H:]
            pa[dx, dy, 0, k] = t01[:HA]
            pa[dx, dy, 1, k] = t01[HA:]
            on = row == col
            both = jnp.where(row < col, t00, jnp.where(on, 0.0, t11))
            d0 = jnp.sum(jnp.where(on, t00, 0.0), axis=0, keepdims=True)
            d1 = jnp.sum(jnp.where(on, t11, 0.0), axis=0, keepdims=True)
            pb[dx, dy, 0, k, :HA] = both[:HA]
            pb[dx, dy, 0, k, HA:] = jnp.broadcast_to(d0, (HB - HA, H))
            pb[dx, dy, 1, k, :HA] = both[HA:]
            pb[dx, dy, 1, k, HA:] = jnp.broadcast_to(d1, (HB - HA, H))

        for part, d, t in ((0, dx, dy), (1, dy, dx)):
            @pl.when(d == 2)
            def _():
                send1(0, part, 2, 0, 0, t)
                send1(0, part, 2, 1, 1, t)

            @pl.when(d == 1)
            def _():
                send1(1, part, 1, 1, 0, t)

            @pl.when(d == 3)
            def _():
                send1(1, part, 3, 0, 1, t)
        return carry

    lax.fori_loop(0, 16, group, 0)

    def each1(kinds, action):
        def step(i, carry):
            for kind in kinds:
                for part in (0, 1):
                    for way in (0, 1):
                        action(level1(kind, part, way, order(i)))
            return carry

        lax.fori_loop(0, 4, step, 0)

    @pl.when(c == 1)
    def _():
        pl.semaphore_wait(turn, 1)
        each1((0,), lambda copy: copy.start())
        each1((1,), lambda copy: copy.start())

    def pass_on(i, carry):
        t = order(i)
        for part in (0, 1):
            for way, d in ((0, 1), (1, 3)):
                level1(0, part, way, t).wait_recv()
                parts, rows = decode(got1.at[0, part, way, t], 512)
                own, diagonals = pieces(place(part, d, t), part, way)
                parts = [a + b for a, b in zip(own, parts)]
                diagonals = {k: diagonals[k] + rows[k] for k in diagonals}
                encode(sent1.at[2, part, way, t], parts, diagonals, 512)
                level1(2, part, way, t).start()
        return carry

    lax.fori_loop(0, 4, pass_on, 0)

    def add_coded(ref, part, half, coded):
        for message in coded:
            parts, rows = decode(message, 512)
            for k in range(NK):
                ref[half, k, :HA] = ref[half, k, :HA] + parts[k]
                if part == 1:
                    ref[half, k, HA:] = ref[half, k, HA:] + rows[k]

    def level2(part, d, pair):
        dev = at(x, (y + d) % NY, z, c) if part == 0 else at((x + d) % NX, y, z, c)
        return remote(
            sent2.at[part, d, pair], got2.at[part, d, pair], l2_s.at[part, d, pair], l2_r.at[part, d, pair], dev
        )

    halves = [(half, n) for half in (0, 1) for n in (0, 1)]

    def far(pair, n):
        return ((z - c + NZ) // 2 + ((2, 3), (1, 0))[pair][n]) % NK

    def send2(part, t, pair):
        ref = place(part, 0, t)
        parts = [ref[half, far(pair, n), :HA] for half, n in halves]
        diagonals = {2 * half + n: ref[half, far(pair, n), HA : HA + 1] for half, n in halves} if part == 1 else {}
        encode(sent2.at[part, t, pair], parts, diagonals, 1024)
        level2(part, t, pair).start()

    def finish1(i, carry):
        t = order(i)
        for part in (0, 1):
            for way in (0, 1):
                level1(1, part, way, t).wait_recv()
                level1(2, part, way, t).wait_recv()
            ref = place(part, 0, t)
            for half in (0, 1):
                add_coded(ref, part, half, (got1.at[2, part, half, t], got1.at[1, part, 1 - half, t]))

            @pl.when(t != 0)
            def _():
                send2(part, t, 0)
        return carry

    lax.fori_loop(0, 4, finish1, 0)

    @pl.when(c == 0)
    def _():
        each1((0, 1), lambda copy: copy.wait_send())
        pl.semaphore_signal(turn, inc=1, device_id=sibling, device_id_type=MESH)

    def second_pair(i, carry):
        for part in (0, 1):
            send2(part, order(i), 1)
        return carry

    lax.fori_loop(0, 3, second_pair, 0)

    def level3(k):
        d = (2 * k + c - z + NZ) % NZ
        return remote(sent3.at[k], got3.at[d], l3_ss.at[k], l3_rs.at[d], at(x, y, 2 * k + c, c))

    def send3(k):
        @pl.when(2 * k + c != z)
        def _():
            parts = [pa[0, 0, 0, k], pa[0, 0, 1, k], pb[0, 0, 0, k, :HA], pb[0, 0, 1, k, :HA]]
            diagonals = {2: pb[0, 0, 0, k, HA : HA + 1], 3: pb[0, 0, 1, k, HA : HA + 1]}
            encode(sent3.at[k], parts, diagonals, 4096)
            level3(k).start()

    for pair in (0, 1):
        for part in (0, 1):
            ref = place(part, 0, 0)
            for d in (1, 3, 2):
                level2(part, d, pair).wait_recv()
                parts, rows = decode(got2.at[part, d, pair], 1024)
                for half, n in halves:
                    k = far(pair, n)
                    ref[half, k, :HA] = ref[half, k, :HA] + parts[2 * half + n]
                    if part == 1:
                        ref[half, k, HA:] = ref[half, k, HA:] + rows[2 * half + n]
        for n in (0, 1):
            send3(far(pair, n))

    owner = z % 2 == c
    xy = x * NY + y
    kz = z // 2

    def ag1(d):
        j = rank((z + d) % NZ, c, kz)
        return remote(gathered.at[c, xy, 0], gathered.at[c, xy, j], ag1_s.at[d], ag1_r.at[j], znb[d])

    @pl.when(owner)
    def _():
        t01a, t01b = pa[0, 0, 0, kz], pa[0, 0, 1, kz]
        ba, bb = pb[0, 0, 0, kz, :HA], pb[0, 0, 1, kz, :HA]
        d0, d1 = pb[0, 0, 0, kz, HA : HA + 1], pb[0, 0, 1, kz, HA : HA + 1]
        def arrive3(d, total):
            remote(got3.at[d], got3.at[d], l3_ss.at[0], l3_rs.at[d], sibling).wait_recv()
            parts, rows = decode(got3.at[d], 4096)
            return tuple(a + b for a, b in zip(total, (*parts, rows[2], rows[3])))

        t01a, t01b, ba, bb, d0, d1 = lax.fori_loop(1, NZ, arrive3, (t01a, t01b, ba, bb, d0, d1))
        scale = 1.0 / TOTAL
        t01 = jnp.concatenate([t01a, t01b], axis=0) * scale
        both = jnp.concatenate([ba, bb], axis=0) * scale
        damp = damping[slot_block[0, dp]]
        d0 = d0 * scale + damp
        d1 = d1 * scale + damp
        flip = both.T
        t00 = jnp.where(row < col, both, jnp.where(row > col, flip, d0))
        t11 = jnp.where(row > col, both, jnp.where(row < col, flip, d1))
        mat = jnp.concatenate(
            [jnp.concatenate([t00, t01], axis=1), jnp.concatenate([t01.T, t11], axis=1)], axis=0
        )
        alpha = 1.0 / jnp.max(jnp.sum(jnp.abs(mat), axis=0, keepdims=True), axis=1, keepdims=True)

        m1, m2, m3 = thirds(mat)

        def times(v):
            v1, v2, v3 = thirds(v)
            a = jnp.dot(jnp.concatenate([v1, v2, v3], axis=0), m1, preferred_element_type=F32)
            b = jnp.dot(jnp.concatenate([v1, v2], axis=0), m2, preferred_element_type=F32)
            e = jnp.dot(v1, m3, preferred_element_type=F32)
            small = a[2 * COLS :] + b[COLS:] + e
            return a[:COLS] + ((a[COLS : 2 * COLS] + b[:COLS]) + small)

        def first(v):
            return 2.0 * alpha * v - alpha * alpha * times(v)

        def second(v):
            p = first(v)
            return 2.0 * p - first(times(p))

        v = second(slab_t[...])
        result = 2.0 * v - second(times(v))
        gathered[c, xy, 0] = result.astype(BF16)
        for d in (1, 7, 4, 3, 5, 2, 6):
            ag1(d).start()

    def sent_exchange(g, carry):
        remote(xs.at[g], xr.at[g], ex_s.at[g], ex_r.at[g], sibling).wait_send()
        return carry

    lax.fori_loop(0, 16, sent_exchange, 0)

    @pl.when(c == 1)
    def _():
        each1((0, 1), lambda copy: copy.wait_send())

    each1((2,), lambda copy: copy.wait_send())
    for part in (0, 1):
        for d in (1, 2, 3):
            for pair in (0, 1):
                level2(part, d, pair).wait_send()
    for k in range(NK):
        @pl.when(2 * k + c != z)
        def _():
            level3(k).wait_send()

    def along(j, e, d):
        even = j % 2 == 0
        return ((x + jnp.where(even, d, e)) % NX) * NY + (y + jnp.where(even, e, d)) % NY

    def whole(j, q, s, r, dev):
        return remote(gathered.at[c, q, j], gathered.at[c, q, j], s, r, dev)

    def ag2(j, d):
        return whole(j, xy, ag_s, ag_r.at[j, xy], (along(j, d, 0) * NZ + z, c))

    def ag3(j, e, d):
        q = along(j, e, 0)
        return whole(j, q, ag_s, ag_r.at[j, q], (along(j, 0, d) * NZ + z, c))

    def landed(j, q):
        whole(j, q, ag_s, ag_r.at[j, q], sibling).wait_recv()

    def forward(cc, j, q):
        return remote(gathered.at[cc, q, j], gathered.at[cc, q, j], fw_s, fw_r, sibling)

    def pass1(j, carry):
        @pl.when(jnp.logical_or(j > 0, jnp.logical_not(owner)))
        def _():
            whole(j, xy, ag1_s.at[0], ag1_r.at[j], sibling).wait_recv()

        for d in (2, 1, 3):
            ag2(j, d).start()
        for d in (2, 1, 3):
            ag3(j, 0, d).start()
        forward(c, j, xy).start()
        return carry

    def pass2(i, carry):
        j, e = i // 3, 2 * (i % 3) + 1 - 3 * ((i % 3) // 2)
        q = along(j, e, 0)
        landed(j, q)
        for d in (2, 1, 3):
            ag3(j, e, d).start()
        forward(c, j, q).start()
        return carry

    def pass3(i, carry):
        for d in (1, 3, 2):
            for e in (0, 1, 3, 2):
                landed(2 * i, along(2 * i, e, d))
            rows = gathered.at[c, pl.ds((x + d) % NX * NY, NY), 2 * i]
            remote(rows, rows, fw_s, fw_r, sibling).start()
        for e in (0, 1, 3, 2):
            for d in (1, 3, 2):
                q = along(2 * i + 1, e, d)
                landed(2 * i + 1, q)
                forward(c, 2 * i + 1, q).start()
        return carry

    lax.fori_loop(0, NK, pass1, 0)
    lax.fori_loop(0, 3 * NK, pass2, 0)
    lax.fori_loop(0, NK // 2, pass3, 0)

    @pl.when(owner)
    def _():
        for d in range(1, NZ):
            ag1(d).wait_send()

    most = gathered.at[c, pl.ds(0, 15)]
    remote(most, most, ag_s, ag_r.at[0, 0], sibling).wait_send()
    remote(gathered.at[c], gathered.at[c], fw_s, fw_r, sibling).wait_send()
    remote(gathered.at[1 - c], gathered.at[1 - c], fw_s, fw_r, sibling).wait_recv()


def permute_kernel(owner_of, gathered, out, sem):
    here = lax.axis_index("dp") % NZ
    nearest = [lax.shift_right_logical(here - plane + NZ, 1) & (NK - 1) for plane in (0, 1)]

    def one(b, carry):
        o = owner_of[b]
        q, plane = lax.shift_right_logical(o, 3), o & 1
        away = (lax.shift_right_logical(o, 1) - jnp.where(plane == 0, *nearest)) & (NK - 1)
        j = away ^ lax.shift_right_logical(away, 1)
        pltpu.make_async_copy(
            gathered.at[plane, q, j], out.at[:, pl.ds(pl.multiple_of(b * B, B), B)], sem
        ).start()
        return carry

    lax.fori_loop(0, OWNERS, one, 0, unroll=8)
    pltpu.make_async_copy(out, out, sem).wait()


def shards(features, grad_slab, damping, owner_of):
    vmem = pl.BlockSpec(memory_space=pltpu.VMEM)
    smem = pl.BlockSpec(memory_space=pltpu.SMEM)
    dma = pltpu.SemaphoreType.DMA
    gathered = pl.pallas_call(
        reduce_kernel,
        out_shape=pltpu.VMEM((2, NX * NY, NK, COLS, B), BF16),
        in_specs=[vmem] + [pl.BlockSpec(memory_space=pl.ANY)] * 3,
        out_specs=vmem,
        scratch_shapes=[
            pltpu.SMEM((1, OWNERS), jnp.int32),
            pltpu.SMEM((OWNERS,), F32),
            pltpu.VMEM((COLS, B), F32),
            pltpu.VMEM((1, OWNERS), jnp.int32),
            pltpu.VMEM((OWNERS, ROWS, B), BF16),
            pltpu.VMEM((16, NK, ROWS, B), BF16),
            pltpu.VMEM((16, NK, ROWS, B), BF16),
            pltpu.VMEM((4, 4, 2, NK, HA, H), F32),
            pltpu.VMEM((4, 4, 2, NK, HB, H), F32),
            pltpu.VMEM((3, 2, 2, 4, CODED, H), jnp.int16),
            pltpu.VMEM((3, 2, 2, 4, CODED, H), jnp.int16),
            pltpu.VMEM((2, 4, 2, CODED, H), jnp.int16),
            pltpu.VMEM((2, 4, 2, CODED, H), jnp.int16),
            pltpu.VMEM((NK, CODED, H), jnp.int16),
            pltpu.VMEM((NZ, CODED, H), jnp.int16),
            pltpu.SemaphoreType.REGULAR, dma((3,)), dma,
            dma((16,)), dma((16,)),
            dma((3, 2, 2, 4)), dma((3, 2, 2, 4)),
            dma((2, 4, 2)), dma((2, 4, 2)),
            dma((NK,)), dma((NZ,)),
            dma((NZ,)), dma((NK,)),
            dma, dma((NK, 16)), dma, dma,
        ],
        compiler_params=pltpu.CompilerParams(
            collective_id=0, has_side_effects=True, vmem_limit_bytes=58 * 1024 * 1024
        ),
    )(owner_of.reshape(1, OWNERS), damping, features, grad_slab.T)
    out = pl.pallas_call(
        permute_kernel,
        out_shape=jax.ShapeDtypeStruct((COLS, OWNERS * B), BF16),
        in_specs=[smem, vmem],
        out_specs=pl.BlockSpec(memory_space=pl.ANY),
        scratch_shapes=[dma],
        compiler_params=pltpu.CompilerParams(vmem_limit_bytes=32 * 1024 * 1024),
    )(owner_of, gathered)
    return out.T


def solution(mesh):
    return jax.shard_map(
        shards,
        mesh=mesh,
        in_specs=(P(("dp", "group"), None), P("dp", None), P(), P()),
        out_specs=P(),
        check_vma=False,
    )
```
